128 devices in a mesh: section: 16 (over x, z_lo, core), tensor: 8 (over y, z_hi).
Axes of the slice: x: 4, y: 4, z: 4 (z_hi: 2, z_lo: 2; z = z_hi * 2 + z_lo), core: 2. Of those that a mesh axis runs over, the one named last changes fastest.
Arguments:
- query_in: bfloat16 [4096, 6144], P('section', 'tensor'), may hold values from -5 to 5
- key_in: bfloat16 [4096, 6144], P('section', 'tensor'), may hold values from -5 to 5
- value_in: bfloat16 [4096, 6144], P('section', 'tensor'), may hold values from -6 to 6
- out_grad: bfloat16 [4096, 6144], P('section', 'tensor'), may hold values from -40 to 40
- group_len: int32 [64], replicated, may hold values from 1 to 64, 3072 in all
Outputs:
- attn_out: bfloat16 [4096, 6144], P(('section', 'tensor'))
- query_grad: bfloat16 [4096, 6144], P(('section', 'tensor'))
- key_grad: bfloat16 [4096, 6144], P(('section', 'tensor'))
- value_grad: bfloat16 [4096, 6144], P(('section', 'tensor'))
The draws below stay inside these ranges and needn't reach their ends.
Inputs may be any that keep to these rules, and one draw needn't show every extreme that they name: Group c holds the tokens at positions c * 64 to c * 64 + group_len[c] - 1; the other slots of its 64 are padding; the lengths sum to 3072.
All inputs are finite; a program needn't handle non-finite values.
Results may differ from the reference program's by a relative error of at most 0.035.
Values may be sent and summed in bfloat16 or wider, within the bound.
A program may use at most 128 MiB of HBM per device.

```python
import math
import jax
import jax.numpy as jnp
import numpy as np
from jax import lax

HEADS = 48
HSIZE = 128
CSLOT = 64
GROUPS = 64
SEQ = 4096
FILLED = 3072


def draw_query_in(key, part):
    key = jax.random.fold_in(key, 11)
    values_base = jnp.clip(jax.random.normal(key, (SEQ, HEADS * HSIZE), jnp.float32), -5.0, 5.0)
    return values_base.astype(jnp.bfloat16)


def draw_key_in(key, part):
    key = jax.random.fold_in(key, 23)
    values_base = jnp.clip(jax.random.normal(key, (SEQ, HEADS * HSIZE), jnp.float32), -5.0, 5.0)
    return values_base.astype(jnp.bfloat16)


def level_of(key, shape, shards, smallest, high):
    def one(dim, shards_of):
        steps = jax.random.uniform(jax.random.fold_in(jax.random.fold_in(key, 6), dim), (shards_of,), jnp.float32, smallest / len(shards), high / len(shards))
        return jnp.repeat(jnp.exp(steps), shape[dim] // shards_of).reshape((-1,) + (1,) * (len(shape) - dim - 1))

    loudness = one(*shards[0])
    for cut in shards[1:]:
        loudness = loudness * one(*cut)
    return loudness


def profile(amount, total, most, slope):
    loads = [(1 << 20) // math.isqrt(rank ** slope) + 1 for rank in range(2, amount + 1)]
    surplus, holding = total - most - (amount - 1), [1] * (amount - 1)
    while surplus > 0:
        candidates = [i for i in range(amount - 1) if holding[i] < most]
        pool, budget = sum([loads[i] for i in candidates]), surplus
        for i in candidates:
            more = min(most - holding[i], max(1, budget * loads[i] // pool), surplus)
            holding[i] = holding[i] + more
            surplus = surplus - more
    return np.array([most] + holding)


def ragged(own_key, count, total, limit, skew):
    if count == 2:
        one = jax.random.randint(own_key, (), max(1, total - limit), min(limit, total - 1) + 1)
        return jnp.stack([one, total - one])
    sizes = jnp.asarray(profile(count, total, limit, skew), jnp.int32)
    pairs = (count - 1) // 2
    donor, taker = sizes[1:1 + 2 * pairs:2], sizes[2:2 + 2 * pairs:2]
    margin = jnp.minimum(donor - 1, limit - taker)
    shifted = jax.random.randint(jax.random.fold_in(own_key, 1), (pairs,), 0, 1 << 20) % (margin + 1)
    sizes = sizes.at[1:1 + 2 * pairs:2].set(donor - shifted).at[2:2 + 2 * pairs:2].set(taker + shifted)
    return sizes[jax.random.permutation(jax.random.fold_in(own_key, 2), count)]


def centred(own_key, extent, scale, limit, cuts=(), kind=jnp.bfloat16):
    drawn = jax.random.normal(own_key, extent, jnp.float32) * scale
    if len(cuts) > 0:
        drawn = level_of(own_key, extent, cuts, -0.22, 0.18) * drawn
    return jnp.clip(drawn, min=-limit, max=limit).astype(kind)


def setup_inputs(seed: int = 0) -> dict:
    streams_of = jax.random.split(jax.random.key(seed), 6)
    query_in = draw_query_in(jax.random.fold_in(streams_of[5], 71), 0)
    key_in = draw_key_in(jax.random.fold_in(streams_of[5], 71), 0)
    value_in = centred(streams_of[2], (SEQ, HEADS * HSIZE), 1.0, 6.0, ((0, 16), (1, 8)))
    out_grad = centred(streams_of[3], (SEQ, HEADS * HSIZE), 8.0, 40.0, ((0, 16), (1, 8)))
    group_len = ragged(streams_of[4], GROUPS, FILLED, CSLOT, 2).astype(jnp.int32)
    return dict(query_in=query_in, key_in=key_in, value_in=value_in, out_grad=out_grad, group_len=group_len)


def reference(query_in, key_in, value_in, out_grad, group_len):
    seq_len = query_in.shape[0]
    positions = jnp.arange(seq_len, dtype=jnp.int32)
    slot_lens = jnp.repeat(group_len, CSLOT, total_repeat_length=seq_len)
    is_valid = positions % CSLOT < slot_lens
    allowed = (positions[None, :] <= positions[:, None]) & is_valid[None, :]
    row_mask = is_valid.astype(jnp.float32)[:, None]
    grad_in = (out_grad.astype(jnp.float32) * row_mask).astype(jnp.bfloat16)
    score_scale = 1.0 / math.sqrt(HSIZE)

    def by_head(matrix):
        return matrix.reshape(seq_len, HEADS, HSIZE).transpose(1, 0, 2)

    def one_head(inputs):
        query_h, key_h, value_h, grad_h = inputs
        scores = jnp.dot(query_h, key_h.T, preferred_element_type=jnp.float32) * score_scale
        scores = jnp.where(allowed, scores, -jnp.inf)
        row_top = lax.optimization_barrier(jnp.max(scores, axis=1, keepdims=True))
        log_total = row_top + jnp.log(lax.optimization_barrier(jnp.sum(jnp.exp(scores - row_top), axis=1, keepdims=True)))
        weights = jnp.exp(scores - log_total)
        weights_low = weights.astype(jnp.bfloat16)
        out_full = jnp.dot(weights_low, value_h, preferred_element_type=jnp.float32)
        row_delta = lax.optimization_barrier(jnp.sum(grad_h.astype(jnp.float32) * out_full, axis=1, keepdims=True))
        grad_scores = jnp.dot(grad_h, value_h.T, preferred_element_type=jnp.float32)
        score_grad = (weights * (grad_scores - row_delta) * score_scale).astype(jnp.bfloat16)
        query_acc = jnp.dot(score_grad, key_h, preferred_element_type=jnp.float32)
        key_acc = jnp.dot(score_grad.T, query_h, preferred_element_type=jnp.float32)
        value_acc = jnp.dot(weights_low.T, grad_h, preferred_element_type=jnp.float32)
        return ((out_full * row_mask).astype(jnp.bfloat16), query_acc.astype(jnp.bfloat16), key_acc.astype(jnp.bfloat16), value_acc.astype(jnp.bfloat16))
    results = lax.map(one_head, (by_head(query_in), by_head(key_in), by_head(value_in), by_head(grad_in)))

    def merged(stack):
        return stack.transpose(1, 0, 2).reshape(seq_len, HEADS * HSIZE)
    return (merged(results[0]), merged(results[1]), merged(results[2]), merged(results[3]))
```

```python
import functools
import math

import jax
import jax.numpy as jnp
from jax import lax
from jax.experimental import pallas as pl
from jax.experimental.pallas import tpu as pltpu
from jax.sharding import PartitionSpec as P

HSIZE = 128
CSLOT = 64
NEG_FILL = -1e30
MESH = pl.DeviceIdType.MESH
F32 = jnp.float32
BF16 = jnp.bfloat16


def chip_of(head, tensor, chips):
    if chips != 8:
        return lax.rem(head + tensor, chips)
    level = head // 3
    x = lax.rem(lax.rem(head, 3) + 2 * level + tensor // 2, 4)
    return 2 * x + level


def head_at(chip, tensor, chips, heads):
    if chips != 8:
        head = lax.rem(chip - lax.rem(tensor, chips) + chips, chips)
        return (head, head < heads)
    level = lax.rem(chip, 2)
    place = lax.rem(chip // 2 + 8 - 2 * level - tensor // 2, 4)
    return (3 * level + place, place < 3)


def dot(a, b, dims):
    return lax.dot_general(a, b, ((dims[:1], dims[1:]), ((), ())), preferred_element_type=F32)


def attention_kernel(
    sections, tensors, heads,
    len_ref, q_ref, k_ref, v_ref, g_ref, out_ref,
    kbuf, vbuf, qbuf, gbuf, kt, vt, bias, ones, sbuf, pbuf, outt, totals, dqt, dk, dv,
    stage, xsend, xrecv,
    recv_sem, fwd_sem, send_sem, fsend_sem, xsend_sem, xrecv_sem, osend_sem, orecv_sem,
):
    rows = q_ref.shape[0]
    half_rows = rows // 2
    chunk = rows // tensors
    half_tensors = tensors // 2
    chips = sections // 2
    blocks = sections // 2
    key_rows = 2 * rows
    score_scale = 1.0 / math.sqrt(HSIZE)
    exp_scale = score_scale * math.log2(math.e)

    me_s = lax.axis_index("section")
    me_t = lax.axis_index("tensor")
    core = lax.rem(me_s, 2)
    sibling = me_s + 1 - 2 * core
    head, active = head_at(me_s // 2, me_t, chips, heads)
    inputs = (k_ref, q_ref, v_ref, g_ref)
    landing = (kbuf, qbuf, vbuf, gbuf)

    def aligned(start, size, step):
        return pl.ds(pl.multiple_of(start, step), size)

    def half_of(section, of_core):
        return lax.rem(of_core + section, 2)

    def key_rows_of(section, half):
        return aligned(section * rows + half * half_rows, half_rows, half_rows)

    def own_rows_of(section):
        return aligned(section * half_rows, half_rows, half_rows)

    def slot(kind, section, half):
        return landing[kind].at[key_rows_of(section, half) if kind in (0, 2) else own_rows_of(section)]

    barrier = pltpu.get_barrier_semaphore()

    @pl.when(active)
    def _():
        @pl.loop(1, sections)
        def _(step):
            pl.semaphore_signal(
                barrier, inc=1, device_id={"section": lax.rem(me_s + step, sections)}, device_id_type=MESH
            )

    out_core = lax.rem(core + me_t // half_tensors, 2)

    @pl.loop(0, tensors)
    def _(tensor):
        @pl.loop(0, heads)
        def _(index):
            target = 2 * chip_of(index, tensor, chips) + out_core

            @pl.when(jnp.logical_or(target != me_s, tensor != me_t))
            def _():
                pl.semaphore_signal(
                    barrier, inc=1, device_id={"section": target, "tensor": tensor}, device_id_type=MESH
                )

    to_itself = me_t < half_tensors
    is_active = active.astype(jnp.int32)
    pl.semaphore_wait(
        barrier,
        2 * heads - is_active + is_active * (sections * half_tensors - to_itself.astype(jnp.int32)),
    )

    for kind in range(4):
        @pl.loop(0, heads)
        def _(step, kind=kind):
            index = lax.rem(step + me_s // 2, heads)
            chip = chip_of(index, me_t, chips)
            for half_step in range(2):
                target_core = core if half_step == 0 else 1 - core
                target = 2 * chip + target_core
                half = half_of(me_s, target_core)
                source = inputs[kind].at[
                    aligned(half * half_rows, half_rows, half_rows), aligned(index * HSIZE, HSIZE, HSIZE)
                ]
                place = slot(kind, me_s, half)

                def send():
                    pltpu.make_async_remote_copy(
                        src_ref=source, dst_ref=place,
                        send_sem=send_sem.at[kind], recv_sem=recv_sem.at[kind, me_s],
                        device_id={"section": target}, device_id_type=MESH,
                    ).start()

                if half_step == 0:
                    @pl.when(target != me_s)
                    def _():
                        send()

                    @pl.when(target == me_s)
                    def _():
                        pltpu.make_async_copy(source, place, recv_sem.at[kind, me_s]).start()
                else:
                    send()

    def wait_arrival(kind, section):
        place = slot(kind, section, half_of(section, core))
        pltpu.make_async_copy(place, place, recv_sem.at[kind, section]).wait()

    def forward(kind):
        which = kind // 2

        @pl.loop(0, sections)
        def _(section):
            wait_arrival(kind, section)
            place = slot(kind, section, half_of(section, core))
            pltpu.make_async_remote_copy(
                src_ref=place, dst_ref=place,
                send_sem=fsend_sem.at[which], recv_sem=fwd_sem.at[which, section],
                device_id={"section": sibling}, device_id_type=MESH,
            ).start()

    def wait_forwarded(kind):
        which = kind // 2

        @pl.loop(0, sections)
        def _(section):
            place = slot(kind, section, half_of(section, 1 - core))
            pltpu.make_async_copy(place, place, fwd_sem.at[which, section]).wait()

    def group_len_of(group):
        return len_ref[group]

    @pl.when(active)
    def _():
        lane = lax.broadcasted_iota(jnp.int32, (CSLOT, HSIZE), 1)
        row = lax.broadcasted_iota(jnp.int32, (CSLOT, HSIZE), 0)

        @pl.loop(0, sections * rows // CSLOT)
        def _(group):
            padded = jnp.logical_and(row >= group_len_of(group), lane == 0)
            bias[aligned(group * CSLOT, CSLOT, CSLOT)] = jnp.where(padded, NEG_FILL, 0.0).astype(BF16)

        ones[...] = jnp.where(
            lax.broadcasted_iota(jnp.int32, ones.shape, 1) == 0, 1.0, 0.0
        ).astype(BF16)

        @pl.loop(0, blocks)
        def _(block):
            span = aligned(block * key_rows, key_rows, key_rows)
            dk[span] = jnp.zeros((key_rows, HSIZE), F32)
            dv[span] = jnp.zeros((key_rows, HSIZE), F32)

        forward(0)

        @pl.loop(0, sections)
        def _(section):
            wait_arrival(1, section)

        forward(2)
        wait_forwarded(0)
        wait_forwarded(2)

        @pl.loop(0, blocks)
        def _(block):
            span = aligned(block * key_rows, key_rows, key_rows)
            kt[:, span] = kbuf[span].T
            vt[:, span] = vbuf[span].T

        def p_span(block, index):
            return aligned((block * (block + 1) // 2 + index) * key_rows, key_rows, key_rows)

        def key_span(index):
            return aligned(index * key_rows, key_rows, key_rows)

        def own_span(block):
            return aligned(block * rows, rows, rows)

        lane_q = lax.broadcasted_iota(jnp.int32, (1, rows), 1)
        query_place = jnp.where(
            lane_q < half_rows, core * half_rows + lane_q, rows + (1 - core) * half_rows + lane_q - half_rows
        )

        @pl.loop(0, blocks)
        def _(block):
            query_wide = jnp.concatenate([qbuf[own_span(block)], ones[...]], axis=1)

            def score_step(index, top, diagonal=False):
                span = key_span(index)
                key_wide = jnp.concatenate([kbuf[span], bias[span]], axis=1)
                scores = dot(key_wide, query_wide, (1, 1))
                if diagonal:
                    place = lax.broadcasted_iota(jnp.int32, (key_rows, rows), 0)
                    scores = jnp.where(place <= query_place, scores, NEG_FILL)
                sbuf[span] = scores
                return jnp.maximum(top, jnp.max(scores.reshape(key_rows // 8, 8, rows), axis=0))

            top = lax.fori_loop(0, block, score_step, jnp.full((8, rows), NEG_FILL, F32))
            top = score_step(block, top, diagonal=True)
            shift = jnp.max(top, axis=0, keepdims=True) * exp_scale
            outt[block] = jnp.zeros((HSIZE, rows), F32)

            def weight_step(index, total):
                span = key_span(index)
                weights = jnp.exp2(sbuf[span] * exp_scale - shift)
                low = weights.astype(BF16)
                pbuf[p_span(block, index)] = low
                outt[block] += dot(vt[:, span], low, (1, 0))
                return total + jnp.sum(weights.reshape(key_rows // 8, 8, rows), axis=0)

            total = lax.fori_loop(0, block + 1, weight_step, jnp.zeros((8, rows), F32))
            totals[block] = jnp.sum(total, axis=0, keepdims=True)

        @pl.loop(0, sections)
        def _(section):
            wait_arrival(3, section)

        def finish(block):
            pltpu.make_async_copy(xrecv.at[block], xrecv.at[block], xrecv_sem.at[block]).wait()
            for unit in range(2):
                mine = key_rows_of(2 * block + unit, half_of(unit, core))
                to = aligned(block * rows + unit * half_rows, half_rows, half_rows)
                part = pl.ds(unit * half_rows, half_rows)
                stage[2, to] = ((dk[mine] + xrecv[block, 0, part].astype(F32)) * score_scale).astype(BF16)
                stage[3, to] = (dv[mine] + xrecv[block, 1, part].astype(F32)).astype(BF16)
            column = aligned((me_t * heads + head) * HSIZE, HSIZE, HSIZE)
            for unit in range(2):
                section = 2 * block + unit

                @pl.loop(0, half_rows // chunk)
                def _(index):
                    tensor = half_of(unit, core) * half_tensors + index
                    source = stage.at[:, aligned(block * rows + unit * half_rows + index * chunk, chunk, chunk)]
                    place = out_ref.at[:, :, column]
                    itself = jnp.logical_and(section == me_s, tensor == me_t)

                    @pl.when(jnp.logical_not(itself))
                    def _():
                        pltpu.make_async_remote_copy(
                            src_ref=source, dst_ref=place, send_sem=osend_sem, recv_sem=orecv_sem,
                            device_id={"section": section, "tensor": tensor}, device_id_type=MESH,
                        ).start()

                    @pl.when(itself)
                    def _():
                        pltpu.make_async_copy(source, place, orecv_sem).start()

        @pl.loop(0, blocks)
        def _(step):
            block = blocks - 1 - step
            own = own_span(block)
            piece = lane_q // CSLOT
            length = jnp.zeros((1, rows), jnp.int32)
            for unit in range(2):
                first = ((2 * block + unit) * rows + half_of(unit, core) * half_rows) // CSLOT
                for inner in range(half_rows // CSLOT):
                    length = jnp.where(
                        piece == unit * (half_rows // CSLOT) + inner, group_len_of(first + inner), length
                    )
            valid = lax.rem(lane_q, CSLOT) < length
            inverse = 1.0 / totals[block]
            keep = jnp.where(valid, inverse, 0.0)
            grad_t = gbuf[own].T.astype(F32) * keep
            out_t = outt[block]
            delta = jnp.sum(grad_t * out_t, axis=0, keepdims=True) * inverse
            stage[0, own] = (out_t * keep).T.astype(BF16)
            grad_low_t = grad_t.astype(BF16)
            grad_low = grad_t.T.astype(BF16)
            query_now = qbuf[own]
            dqt[...] = jnp.zeros((HSIZE, rows), F32)

            def grad_step(index, _):
                span = key_span(index)
                low = pbuf[p_span(block, index)]
                grad_scores = dot(vbuf[span], grad_low_t, (1, 0))
                score_grad = (low.astype(F32) * (grad_scores - delta)).astype(BF16)
                dv[span] += dot(low, grad_low, (1, 0))
                dk[span] += dot(score_grad, query_now, (1, 0))
                dqt[...] += dot(kt[:, span], score_grad, (1, 0))
                return 0

            lax.fori_loop(0, block + 1, grad_step, 0)
            stage[1, own] = (dqt[...] * score_scale).T.astype(BF16)
            for unit in range(2):
                theirs = key_rows_of(2 * block + unit, half_of(unit, 1 - core))
                part = pl.ds(unit * half_rows, half_rows)
                xsend[block, 0, part] = dk[theirs].astype(BF16)
                xsend[block, 1, part] = dv[theirs].astype(BF16)
            pltpu.make_async_remote_copy(
                src_ref=xsend.at[block], dst_ref=xrecv.at[block],
                send_sem=xsend_sem, recv_sem=xrecv_sem.at[block],
                device_id={"section": sibling}, device_id_type=MESH,
            ).start()

            @pl.when(step > 0)
            def _():
                finish(block + 1)

        finish(0)

        for kind in (0, 2):
            part = landing[kind].at[pl.ds(0, sections * half_rows)]
            pltpu.make_async_copy(part, part, fsend_sem.at[kind // 2]).wait()
        pltpu.make_async_copy(xsend, xsend, xsend_sem).wait()

        @pl.when(to_itself)
        def _():
            part = stage.at[:, pl.ds(0, sections * half_rows - chunk)]
            pltpu.make_async_copy(part, part, osend_sem).wait()

        @pl.when(jnp.logical_not(to_itself))
        def _():
            pltpu.make_async_copy(stage, stage, osend_sem).wait()

        for kind in range(4):
            part = vbuf.at[pl.ds(0, (2 * heads - 1) * half_rows)]
            pltpu.make_async_copy(part, part, send_sem.at[kind]).wait()

    @pl.when(jnp.logical_not(active))
    def _():
        for kind in range(4):
            part = vbuf.at[pl.ds(0, 2 * heads * half_rows)]
            pltpu.make_async_copy(part, part, send_sem.at[kind]).wait()

    pltpu.make_async_copy(out_ref, out_ref, orecv_sem).wait()


def per_device(query_in, key_in, value_in, out_grad, group_len):
    rows, columns = query_in.shape
    sections, tensors = lax.axis_size("section"), lax.axis_size("tensor")
    heads = columns // HSIZE
    chunk = rows // tensors
    seq_len = rows * sections
    own = seq_len // 2
    blocks = sections // 2
    tiles = blocks * (blocks + 1) // 2
    vmem = pltpu.VMEM
    dma = pltpu.SemaphoreType.DMA
    anywhere = pl.BlockSpec(memory_space=pl.ANY)
    out = pl.pallas_call(
        functools.partial(attention_kernel, sections, tensors, heads),
        out_shape=jax.ShapeDtypeStruct((4, chunk, columns * tensors), BF16),
        in_specs=[pl.BlockSpec(memory_space=pltpu.SMEM)] + [anywhere] * 4,
        out_specs=anywhere,
        scratch_shapes=[
            vmem((seq_len, HSIZE), BF16),
            vmem((seq_len, HSIZE), BF16),
            vmem((own, HSIZE), BF16),
            vmem((own, HSIZE), BF16),
            vmem((HSIZE, seq_len), BF16),
            vmem((HSIZE, seq_len), BF16),
            vmem((seq_len, HSIZE), BF16),
            vmem((rows, HSIZE), BF16),
            vmem((seq_len, rows), F32),
            vmem((tiles * 2 * rows, rows), BF16),
            vmem((blocks, HSIZE, rows), F32),
            vmem((blocks, 1, rows), F32),
            vmem((HSIZE, rows), F32),
            vmem((seq_len, HSIZE), F32),
            vmem((seq_len, HSIZE), F32),
            vmem((4, own, HSIZE), BF16),
            vmem((blocks, 2, rows, HSIZE), BF16),
            vmem((blocks, 2, rows, HSIZE), BF16),
            dma((4, sections)),
            dma((2, sections)),
            dma((4,)),
            dma((2,)),
            dma,
            dma((blocks,)),
            dma,
            dma,
        ],
        compiler_params=pltpu.CompilerParams(
            collective_id=0, has_side_effects=True, vmem_limit_bytes=56 * 1024 * 1024
        ),
        cost_estimate=pl.CostEstimate(
            flops=12 * HSIZE * seq_len * seq_len // 4,
            bytes_accessed=16 * rows * columns,
            transcendentals=seq_len * seq_len // 4,
        ),
    )(group_len, query_in, key_in, value_in, out_grad)
    return tuple(out[index] for index in range(4))


def solution(mesh):
    whole = P(("section", "tensor"), None)
    return jax.shard_map(
        per_device,
        mesh=mesh,
        in_specs=(P("section", "tensor"),) * 4 + (P(),),
        out_specs=(whole,) * 4,
        check_vma=False,
    )
```

```python
import functools
import math

import jax
import jax.numpy as jnp
from jax import lax
from jax.experimental import pallas as pl
from jax.experimental.pallas import tpu as pltpu
from jax.sharding import PartitionSpec as P

HSIZE = 128
CSLOT = 64
NEG_FILL = -1e30
MESH = pl.DeviceIdType.MESH
F32 = jnp.float32
BF16 = jnp.bfloat16


def chip_of(head, tensor, chips):
    if chips != 8:
        return lax.rem(head + tensor, chips)
    level = head // 4
    x = lax.rem((1 + level) * lax.rem(head, 4) + tensor // 2, 4)
    return 2 * x + level


def head_at(chip, tensor, chips, heads):
    if chips != 8:
        head = lax.rem(chip - lax.rem(tensor, chips) + chips, chips)
        return (head, head < heads)
    level = lax.rem(chip, 2)
    place = lax.rem(chip // 2 + 4 - tensor // 2, 4)
    return (
        jnp.where(level == 0, place, 4 + place // 2),
        jnp.logical_or(level == 0, lax.rem(place, 2) == 0),
    )


def dot(a, b, dims):
    return lax.dot_general(a, b, ((dims[:1], dims[1:]), ((), ())), preferred_element_type=F32)


def attention_kernel(
    sections, tensors, heads,
    len_ref, q_ref, k_ref, v_ref, g_ref, out_ref,
    kbuf, vbuf, qbuf, gbuf, kt, vt, bias, ones, sbuf, pbuf, outt, tops, totals, dqt, dk, dv,
    stage, xsend, xrecv,
    recv_sem, fwd_sem, send_sem, fsend_sem, xsend_sem, xrecv_sem, osend_sem, orecv_sem, entered,
):
    rows = q_ref.shape[0]
    half_rows = rows // 2
    chunk = rows // tensors
    half_tensors = tensors // 2
    chips = sections // 2
    blocks = sections // 2
    key_rows = 2 * rows
    score_scale = 1.0 / math.sqrt(HSIZE)
    exp_scale = score_scale * math.log2(math.e)

    me_s = lax.axis_index("section")
    me_t = lax.axis_index("tensor")
    core = lax.rem(me_s, 2)
    sibling = me_s + 1 - 2 * core
    head, active = head_at(me_s // 2, me_t, chips, heads)
    inputs = (k_ref, q_ref, v_ref, g_ref)
    landing = (kbuf, qbuf, vbuf, gbuf)

    def aligned(start, size, step):
        return pl.ds(pl.multiple_of(start, step), size)

    def half_of(section, of_core):
        return lax.rem(of_core + section, 2)

    def key_rows_of(section, half):
        return aligned(section * rows + half * half_rows, half_rows, half_rows)

    def own_rows_of(section):
        return aligned(section * half_rows, half_rows, half_rows)

    def slot(kind, section, half):
        return landing[kind].at[key_rows_of(section, half) if kind in (0, 2) else own_rows_of(section)]

    barrier = pltpu.get_barrier_semaphore()
    steps = [1 << bit for bit in range(tensors.bit_length() - 1)]
    for step in range(1, sections):
        pl.semaphore_signal(
            barrier, inc=1, device_id={"section": jnp.bitwise_xor(me_s, step)}, device_id_type=MESH
        )
    for step in steps:
        pl.semaphore_signal(
            barrier, inc=1, device_id={"tensor": jnp.bitwise_xor(me_t, step)}, device_id_type=MESH
        )
    pl.semaphore_wait(barrier, sections - 1 + len(steps))

    for kind in range(4):
        @pl.loop(0, heads)
        def _(step, kind=kind):
            index = lax.rem(step + me_s // 2, heads)
            chip = chip_of(index, me_t, chips)
            for half_step in range(2):
                target_core = core if half_step == 0 else 1 - core
                target = 2 * chip + target_core
                half = half_of(me_s, target_core)
                source = inputs[kind].at[
                    aligned(half * half_rows, half_rows, half_rows), aligned(index * HSIZE, HSIZE, HSIZE)
                ]
                place = slot(kind, me_s, half)

                def send():
                    pltpu.make_async_remote_copy(
                        src_ref=source, dst_ref=place,
                        send_sem=send_sem.at[kind], recv_sem=recv_sem.at[kind, me_s],
                        device_id={"section": target}, device_id_type=MESH,
                    ).start()

                if half_step == 0:
                    @pl.when(target != me_s)
                    def _():
                        send()

                    @pl.when(target == me_s)
                    def _():
                        pltpu.make_async_copy(source, place, recv_sem.at[kind, me_s]).start()
                else:
                    send()

    def wait_arrival(kind, section):
        place = slot(kind, section, half_of(section, core))
        pltpu.make_async_copy(place, place, recv_sem.at[kind, section]).wait()

    def forward(kind):
        which = kind // 2

        @pl.loop(0, sections)
        def _(section):
            wait_arrival(kind, section)
            place = slot(kind, section, half_of(section, core))
            pltpu.make_async_remote_copy(
                src_ref=place, dst_ref=place,
                send_sem=fsend_sem.at[which], recv_sem=fwd_sem.at[which, section],
                device_id={"section": sibling}, device_id_type=MESH,
            ).start()

    def wait_forwarded(kind):
        which = kind // 2

        @pl.loop(0, sections)
        def _(section):
            place = slot(kind, section, half_of(section, 1 - core))
            pltpu.make_async_copy(place, place, fwd_sem.at[which, section]).wait()

    def group_len_of(group):
        return len_ref[group]

    for bit, step in enumerate(steps):
        pl.semaphore_signal(
            entered.at[bit], inc=1, device_id={"tensor": jnp.bitwise_xor(me_t, step)}, device_id_type=MESH
        )
        pl.semaphore_wait(entered.at[bit], 1)

    to_itself = me_t < half_tensors

    @pl.when(active)
    def _():
        lane = lax.broadcasted_iota(jnp.int32, (CSLOT, HSIZE), 1)
        row = lax.broadcasted_iota(jnp.int32, (CSLOT, HSIZE), 0)

        @pl.loop(0, sections * rows // CSLOT)
        def _(group):
            padded = jnp.logical_and(row >= group_len_of(group), lane == 0)
            bias[aligned(group * CSLOT, CSLOT, CSLOT)] = jnp.where(padded, NEG_FILL, 0.0).astype(BF16)

        ones[...] = jnp.where(
            lax.broadcasted_iota(jnp.int32, ones.shape, 1) == 0, 1.0, 0.0
        ).astype(BF16)

        @pl.loop(0, blocks)
        def _(block):
            span = aligned(block * key_rows, key_rows, key_rows)
            dk[span] = jnp.zeros((key_rows, HSIZE), F32)
            dv[span] = jnp.zeros((key_rows, HSIZE), F32)

        forward(0)

        @pl.loop(0, sections)
        def _(section):
            wait_arrival(1, section)

        wait_forwarded(0)

        def p_span(block, index):
            return aligned((block * (block + 1) // 2 + index) * key_rows, key_rows, key_rows)

        def key_span(index):
            return aligned(index * key_rows, key_rows, key_rows)

        def own_span(block):
            return aligned(block * rows, rows, rows)

        lane_q = lax.broadcasted_iota(jnp.int32, (1, rows), 1)
        query_place = jnp.where(
            lane_q < half_rows, core * half_rows + lane_q, rows + (1 - core) * half_rows + lane_q - half_rows
        )

        def send_out(block, first, last, group):
            column = aligned((me_t * heads + head) * HSIZE, HSIZE, HSIZE)
            for unit in range(2):
                section = 2 * block + unit

                @pl.loop(0, half_rows // chunk)
                def _(index):
                    tensor = half_of(unit, core) * half_tensors + index
                    start = block * rows + unit * half_rows + index * chunk
                    source = stage.at[pl.ds(first, last - first), aligned(start, chunk, chunk)]
                    place = out_ref.at[pl.ds(first, last - first), :, column]
                    itself = jnp.logical_and(section == me_s, tensor == me_t)

                    @pl.when(jnp.logical_not(itself))
                    def _():
                        pltpu.make_async_remote_copy(
                            src_ref=source, dst_ref=place,
                            send_sem=osend_sem.at[group], recv_sem=orecv_sem.at[group],
                            device_id={"section": section, "tensor": tensor}, device_id_type=MESH,
                        ).start()

                    @pl.when(itself)
                    def _():
                        pltpu.make_async_copy(source, place, orecv_sem.at[group]).start()

        def valid_rows(block):
            piece = lane_q // CSLOT
            length = jnp.zeros((1, rows), jnp.int32)
            for unit in range(2):
                first = ((2 * block + unit) * rows + half_of(unit, core) * half_rows) // CSLOT
                for inner in range(half_rows // CSLOT):
                    length = jnp.where(
                        piece == unit * (half_rows // CSLOT) + inner, group_len_of(first + inner), length
                    )
            return lax.rem(lane_q, CSLOT) < length

        @pl.loop(0, blocks)
        def _(block):
            span = key_span(block)
            kt[:, span] = kbuf[span].T
            query_wide = jnp.concatenate([qbuf[own_span(block)], ones[...]], axis=1)

            def score_step(index, top, diagonal=False):
                span = key_span(index)
                key_wide = jnp.concatenate([kbuf[span], bias[span]], axis=1)
                scores = dot(key_wide, query_wide, (1, 1))
                if diagonal:
                    place = lax.broadcasted_iota(jnp.int32, (key_rows, rows), 0)
                    scores = jnp.where(place <= query_place, scores, NEG_FILL)
                sbuf[p_span(block, index)] = scores
                return jnp.maximum(top, jnp.max(scores.reshape(key_rows // 8, 8, rows), axis=0))

            top = lax.fori_loop(0, block, score_step, jnp.full((8, rows), NEG_FILL, F32))
            tops[block] = score_step(block, top, diagonal=True)

        forward(2)
        wait_forwarded(2)

        @pl.loop(0, blocks)
        def _(block):
            span = key_span(block)
            vt[:, span] = vbuf[span].T
            shift = jnp.max(tops[block], axis=0, keepdims=True) * exp_scale
            outt[block] = jnp.zeros((HSIZE, rows), F32)

            def weight_step(index, total):
                weights = jnp.exp2(sbuf[p_span(block, index)] * exp_scale - shift)
                low = weights.astype(BF16)
                pbuf[p_span(block, index)] = low
                outt[block] += dot(vt[:, key_span(index)], low, (1, 0))
                return total + jnp.sum(weights.reshape(key_rows // 8, 8, rows), axis=0)

            total = lax.fori_loop(0, block + 1, weight_step, jnp.zeros((8, rows), F32))
            total = jnp.sum(total, axis=0, keepdims=True)
            totals[block] = total
            keep = jnp.where(valid_rows(block), 1.0 / total, 0.0)
            stage[0, own_span(block)] = (outt[block] * keep).T.astype(BF16)
            send_out(block, 0, 1, 0)

        @pl.loop(0, sections)
        def _(section):
            wait_arrival(3, section)

        def finish(block):
            pltpu.make_async_copy(xrecv.at[block], xrecv.at[block], xrecv_sem.at[block]).wait()
            for unit in range(2):
                mine = key_rows_of(2 * block + unit, half_of(unit, core))
                to = aligned(block * rows + unit * half_rows, half_rows, half_rows)
                part = pl.ds(unit * half_rows, half_rows)
                stage[2, to] = ((dk[mine] + xrecv[block, 0, part].astype(F32)) * score_scale).astype(BF16)
                stage[3, to] = (dv[mine] + xrecv[block, 1, part].astype(F32)).astype(BF16)
            send_out(block, 1, 4, 1)

        @pl.loop(0, blocks)
        def _(step):
            block = blocks - 1 - step
            own = own_span(block)
            inverse = 1.0 / totals[block]
            keep = jnp.where(valid_rows(block), inverse, 0.0)
            grad_t = gbuf[own].T.astype(F32) * keep
            out_t = outt[block]
            delta = jnp.sum(grad_t * out_t, axis=0, keepdims=True) * inverse
            grad_low_t = grad_t.astype(BF16)
            grad_low = grad_t.T.astype(BF16)
            query_now = qbuf[own]
            dqt[...] = jnp.zeros((HSIZE, rows), F32)

            def grad_step(index, _):
                span = key_span(index)
                low = pbuf[p_span(block, index)]
                grad_scores = dot(vbuf[span], grad_low_t, (1, 0))
                score_grad = (low.astype(F32) * (grad_scores - delta)).astype(BF16)
                dv[span] += dot(low, grad_low, (1, 0))
                dk[span] += dot(score_grad, query_now, (1, 0))
                dqt[...] += dot(kt[:, span], score_grad, (1, 0))
                return 0

            lax.fori_loop(0, block + 1, grad_step, 0)
            stage[1, own] = (dqt[...] * score_scale).T.astype(BF16)
            for unit in range(2):
                theirs = key_rows_of(2 * block + unit, half_of(unit, 1 - core))
                part = pl.ds(unit * half_rows, half_rows)
                xsend[block, 0, part] = dk[theirs].astype(BF16)
                xsend[block, 1, part] = dv[theirs].astype(BF16)
            pltpu.make_async_remote_copy(
                src_ref=xsend.at[block], dst_ref=xrecv.at[block],
                send_sem=xsend_sem, recv_sem=xrecv_sem.at[block],
                device_id={"section": sibling}, device_id_type=MESH,
            ).start()

            @pl.when(step > 0)
            def _():
                finish(block + 1)

        finish(0)

        for kind in (0, 2):
            part = landing[kind].at[pl.ds(0, sections * half_rows)]
            pltpu.make_async_copy(part, part, fsend_sem.at[kind // 2]).wait()
        pltpu.make_async_copy(xsend, xsend, xsend_sem).wait()

        own_rows = sections * half_rows
        for group, (first, last) in enumerate(((0, 1), (1, 4))):
            @pl.when(to_itself)
            def _():
                part = stage.at[pl.ds(first, last - first), pl.ds(0, own_rows - chunk)]
                pltpu.make_async_copy(part, part, osend_sem.at[group]).wait()

            @pl.when(jnp.logical_not(to_itself))
            def _():
                part = stage.at[pl.ds(first, last - first)]
                pltpu.make_async_copy(part, part, osend_sem.at[group]).wait()

        for kind in range(4):
            part = vbuf.at[pl.ds(0, (2 * heads - 1) * half_rows)]
            pltpu.make_async_copy(part, part, send_sem.at[kind]).wait()

    @pl.when(jnp.logical_not(active))
    def _():
        for kind in range(4):
            part = vbuf.at[pl.ds(0, 2 * heads * half_rows)]
            pltpu.make_async_copy(part, part, send_sem.at[kind]).wait()

    for group, (first, last) in enumerate(((0, 1), (1, 4))):
        part = out_ref.at[pl.ds(first, last - first)]
        pltpu.make_async_copy(part, part, orecv_sem.at[group]).wait()


def per_device(query_in, key_in, value_in, out_grad, group_len):
    rows, columns = query_in.shape
    sections, tensors = lax.axis_size("section"), lax.axis_size("tensor")
    heads = columns // HSIZE
    chunk = rows // tensors
    seq_len = rows * sections
    own = seq_len // 2
    blocks = sections // 2
    tiles = blocks * (blocks + 1) // 2
    vmem = pltpu.VMEM
    dma = pltpu.SemaphoreType.DMA
    anywhere = pl.BlockSpec(memory_space=pl.ANY)
    out = pl.pallas_call(
        functools.partial(attention_kernel, sections, tensors, heads),
        out_shape=jax.ShapeDtypeStruct((4, chunk, columns * tensors), BF16),
        in_specs=[pl.BlockSpec(memory_space=pltpu.SMEM)] + [anywhere] * 4,
        out_specs=anywhere,
        scratch_shapes=[
            vmem((seq_len, HSIZE), BF16),
            vmem((seq_len, HSIZE), BF16),
            vmem((own, HSIZE), BF16),
            vmem((own, HSIZE), BF16),
            vmem((HSIZE, seq_len), BF16),
            vmem((HSIZE, seq_len), BF16),
            vmem((seq_len, HSIZE), BF16),
            vmem((rows, HSIZE), BF16),
            vmem((tiles * 2 * rows, rows), F32),
            vmem((tiles * 2 * rows, rows), BF16),
            vmem((blocks, HSIZE, rows), F32),
            vmem((blocks, 8, rows), F32),
            vmem((blocks, 1, rows), F32),
            vmem((HSIZE, rows), F32),
            vmem((seq_len, HSIZE), F32),
            vmem((seq_len, HSIZE), F32),
            vmem((4, own, HSIZE), BF16),
            vmem((blocks, 2, rows, HSIZE), BF16),
            vmem((blocks, 2, rows, HSIZE), BF16),
            dma((4, sections)),
            dma((2, sections)),
            dma((4,)),
            dma((2,)),
            dma,
            dma((blocks,)),
            dma((2,)),
            dma((2,)),
            pltpu.SemaphoreType.REGULAR((tensors.bit_length() - 1,)),
        ],
        compiler_params=pltpu.CompilerParams(
            collective_id=0, has_side_effects=True, vmem_limit_bytes=56 * 1024 * 1024
        ),
        cost_estimate=pl.CostEstimate(
            flops=12 * HSIZE * seq_len * seq_len // 4,
            bytes_accessed=16 * rows * columns,
            transcendentals=seq_len * seq_len // 4,
        ),
    )(group_len, query_in, key_in, value_in, out_grad)
    return tuple(out[index] for index in range(4))


def solution(mesh):
    whole = P(("section", "tensor"), None)
    return jax.shard_map(
        per_device,
        mesh=mesh,
        in_specs=(P("section", "tensor"),) * 4 + (P(),),
        out_specs=(whole,) * 4,
        check_vma=False,
    )
```

```python
import functools
import math

import jax
import jax.numpy as jnp
from jax import lax
from jax.experimental import pallas as pl
from jax.experimental.pallas import tpu as pltpu
from jax.sharding import PartitionSpec as P

HSIZE = 128
CSLOT = 64
NEG_FILL = -1e30
MESH = pl.DeviceIdType.MESH
F32 = jnp.float32
BF16 = jnp.bfloat16


def chip_of(head, tensor, chips):
    if chips != 8:
        return lax.rem(head + tensor, chips)
    level = head // 4
    x = lax.rem((1 + level) * lax.rem(head, 4) + tensor // 2, 4)
    return 2 * x + level


def head_at(chip, tensor, chips, heads):
    if chips != 8:
        head = lax.rem(chip - lax.rem(tensor, chips) + chips, chips)
        return (head, head < heads)
    level = lax.rem(chip, 2)
    place = lax.rem(chip // 2 + 4 - tensor // 2, 4)
    return (
        jnp.where(level == 0, place, 4 + place // 2),
        jnp.logical_or(level == 0, lax.rem(place, 2) == 0),
    )


def dot(a, b, dims):
    return lax.dot_general(a, b, ((dims[:1], dims[1:]), ((), ())), preferred_element_type=F32)


def attention_kernel(
    sections, tensors, heads,
    len_ref, q_ref, k_ref, v_ref, g_ref, out_ref,
    kbuf, vbuf, qbuf, gbuf, kt, vt, bias, ones, sbuf, pbuf, outt, tops, totals, dk, dv,
    stage, xsend, xrecv,
    recv_sem, fwd_sem, send_sem, fsend_sem, xsend_sem, xrecv_sem, osend_sem, orecv_sem, entered,
):
    rows = q_ref.shape[0]
    half_rows = rows // 2
    chunk = rows // tensors
    half_tensors = tensors // 2
    chips = sections // 2
    blocks = sections // 2
    key_rows = 2 * rows
    score_scale = 1.0 / math.sqrt(HSIZE)
    exp_scale = score_scale * math.log2(math.e)

    me_s = lax.axis_index("section")
    me_t = lax.axis_index("tensor")
    core = lax.rem(me_s, 2)
    sibling = me_s + 1 - 2 * core
    head, active = head_at(me_s // 2, me_t, chips, heads)
    inputs = (k_ref, q_ref, v_ref, g_ref)
    landing = (kbuf, qbuf, vbuf, gbuf)

    def aligned(start, size, step):
        return pl.ds(pl.multiple_of(start, step), size)

    def half_of(section, of_core):
        return lax.rem(of_core + section, 2)

    def key_rows_of(section, half):
        return aligned(section * rows + half * half_rows, half_rows, half_rows)

    def own_rows_of(section):
        return aligned(section * half_rows, half_rows, half_rows)

    def slot(kind, section, half):
        return landing[kind].at[key_rows_of(section, half) if kind in (0, 2) else own_rows_of(section)]

    barrier = pltpu.get_barrier_semaphore()
    steps = [1 << bit for bit in range(tensors.bit_length() - 1)]
    for step in range(1, sections):
        pl.semaphore_signal(
            barrier, inc=1, device_id={"section": jnp.bitwise_xor(me_s, step)}, device_id_type=MESH
        )
    for step in steps:
        pl.semaphore_signal(
            barrier, inc=1, device_id={"tensor": jnp.bitwise_xor(me_t, step)}, device_id_type=MESH
        )
    pl.semaphore_wait(barrier, sections - 1 + len(steps))

    def send_kind(kind):
        @pl.loop(0, heads)
        def _(step):
            index = lax.rem(step + me_s // 2, heads)
            chip = chip_of(index, me_t, chips)
            for half_step in range(2):
                target_core = core if half_step == 0 else 1 - core
                target = 2 * chip + target_core
                half = half_of(me_s, target_core)
                source = inputs[kind].at[
                    aligned(half * half_rows, half_rows, half_rows), aligned(index * HSIZE, HSIZE, HSIZE)
                ]
                place = slot(kind, me_s, half)

                def send():
                    pltpu.make_async_remote_copy(
                        src_ref=source, dst_ref=place,
                        send_sem=send_sem.at[kind], recv_sem=recv_sem.at[kind, me_s],
                        device_id={"section": target}, device_id_type=MESH,
                    ).start()

                if half_step == 0:
                    @pl.when(target != me_s)
                    def _():
                        send()

                    @pl.when(target == me_s)
                    def _():
                        pltpu.make_async_copy(source, place, recv_sem.at[kind, me_s]).start()
                else:
                    send()

    def wait_sent(kind):
        @pl.when(active)
        def _():
            part = vbuf.at[pl.ds(0, (2 * heads - 1) * half_rows)]
            pltpu.make_async_copy(part, part, send_sem.at[kind]).wait()

        @pl.when(jnp.logical_not(active))
        def _():
            part = vbuf.at[pl.ds(0, 2 * heads * half_rows)]
            pltpu.make_async_copy(part, part, send_sem.at[kind]).wait()

    def wait_arrival(kind, section):
        place = slot(kind, section, half_of(section, core))
        pltpu.make_async_copy(place, place, recv_sem.at[kind, section]).wait()

    def forward(kind):
        which = kind // 2

        @pl.loop(0, sections)
        def _(section):
            wait_arrival(kind, section)
            place = slot(kind, section, half_of(section, core))
            pltpu.make_async_remote_copy(
                src_ref=place, dst_ref=place,
                send_sem=fsend_sem.at[which], recv_sem=fwd_sem.at[which, section],
                device_id={"section": sibling}, device_id_type=MESH,
            ).start()

    def wait_forwarded(kind):
        which = kind // 2

        @pl.loop(0, sections)
        def _(section):
            place = slot(kind, section, half_of(section, 1 - core))
            pltpu.make_async_copy(place, place, fwd_sem.at[which, section]).wait()

    send_kind(0)
    send_kind(1)
    wait_sent(0)
    send_kind(2)

    def group_len_of(group):
        return len_ref[group]

    for bit, step in enumerate(steps):
        pl.semaphore_signal(
            entered.at[bit], inc=1, device_id={"tensor": jnp.bitwise_xor(me_t, step)}, device_id_type=MESH
        )
        pl.semaphore_wait(entered.at[bit], 1)

    to_itself = me_t < half_tensors

    @pl.when(active)
    def _():
        lane = lax.broadcasted_iota(jnp.int32, (CSLOT, HSIZE), 1)
        row = lax.broadcasted_iota(jnp.int32, (CSLOT, HSIZE), 0)

        @pl.loop(0, sections * rows // CSLOT)
        def _(group):
            padded = jnp.logical_and(row >= group_len_of(group), lane == 0)
            bias[aligned(group * CSLOT, CSLOT, CSLOT)] = jnp.where(padded, NEG_FILL, 0.0).astype(BF16)

        ones[...] = jnp.where(
            lax.broadcasted_iota(jnp.int32, ones.shape, 1) == 0, 1.0, 0.0
        ).astype(BF16)

        forward(0)

    wait_sent(1)
    send_kind(3)

    @pl.when(active)
    def _():
        @pl.loop(0, sections)
        def _(section):
            wait_arrival(1, section)

        wait_forwarded(0)

        def p_span(block, index, count=1):
            return pl.ds((block * (block + 1) // 2 + index) * key_rows, count * key_rows)

        def key_span(index, count=1):
            return pl.ds(index * key_rows, count * key_rows)

        def own_span(block):
            return pl.ds(block * rows, rows)

        lane_q = lax.broadcasted_iota(jnp.int32, (1, rows), 1)
        query_place = jnp.where(
            lane_q < half_rows, core * half_rows + lane_q, rows + (1 - core) * half_rows + lane_q - half_rows
        )

        def send_out(block, first, last, group):
            column = aligned((me_t * heads + head) * HSIZE, HSIZE, HSIZE)
            for unit in range(2):
                section = 2 * block + unit

                @pl.loop(0, half_rows // chunk)
                def _(index):
                    tensor = half_of(unit, core) * half_tensors + index
                    start = block * rows + unit * half_rows + index * chunk
                    source = stage.at[pl.ds(first, last - first), aligned(start, chunk, chunk)]
                    place = out_ref.at[pl.ds(first, last - first), :, column]
                    itself = jnp.logical_and(section == me_s, tensor == me_t)

                    @pl.when(jnp.logical_not(itself))
                    def _():
                        pltpu.make_async_remote_copy(
                            src_ref=source, dst_ref=place,
                            send_sem=osend_sem.at[group], recv_sem=orecv_sem.at[group],
                            device_id={"section": section, "tensor": tensor}, device_id_type=MESH,
                        ).start()

                    @pl.when(itself)
                    def _():
                        pltpu.make_async_copy(source, place, orecv_sem.at[group]).start()

        def valid_rows(block):
            piece = lane_q // CSLOT
            length = jnp.zeros((1, rows), jnp.int32)
            for unit in range(2):
                first = ((2 * block + unit) * rows + half_of(unit, core) * half_rows) // CSLOT
                for inner in range(half_rows // CSLOT):
                    length = jnp.where(
                        piece == unit * (half_rows // CSLOT) + inner, group_len_of(first + inner), length
                    )
            return lax.rem(lane_q, CSLOT) < length

        for block in range(blocks):
            span = key_span(block)
            kt[:, span] = kbuf[span].T
            query_wide = jnp.concatenate([qbuf[own_span(block)], ones[...]], axis=1)

            top = jnp.full((8, rows), NEG_FILL, F32)
            for index in range(block + 1):
                span = key_span(index)
                key_wide = jnp.concatenate([kbuf[span], bias[span]], axis=1)
                scores = dot(key_wide, query_wide, (1, 1))
                if index == block:
                    place = lax.broadcasted_iota(jnp.int32, (key_rows, rows), 0)
                    scores = jnp.where(place <= query_place, scores, NEG_FILL)
                sbuf[p_span(block, index)] = scores
                top = jnp.maximum(top, jnp.max(scores.reshape(key_rows // 8, 8, rows), axis=0))
            tops[block] = top

        forward(2)
        wait_forwarded(2)

        for block in range(blocks):
            span = key_span(block)
            vt[:, span] = vbuf[span].T
            shift = jnp.max(tops[block], axis=0, keepdims=True) * exp_scale
            weights = jnp.exp2(sbuf[p_span(block, 0, block + 1)] * exp_scale - shift)
            low = weights.astype(BF16)
            pbuf[p_span(block, 0, block + 1)] = low
            total = jnp.sum(weights, axis=0, keepdims=True)
            totals[block] = total
            out_t = dot(vt[:, key_span(0, block + 1)], low, (1, 0))
            outt[block] = out_t
            keep = jnp.where(valid_rows(block), 1.0 / total, 0.0)
            stage[0, own_span(block)] = (out_t * keep).T.astype(BF16)
            send_out(block, 0, 1, 0)

        @pl.loop(0, sections)
        def _(section):
            wait_arrival(3, section)

        def finish(block):
            pltpu.make_async_copy(xrecv.at[block], xrecv.at[block], xrecv_sem.at[block]).wait()
            for unit in range(2):
                mine = key_rows_of(2 * block + unit, half_of(unit, core))
                to = aligned(block * rows + unit * half_rows, half_rows, half_rows)
                part = pl.ds(unit * half_rows, half_rows)
                stage[2, to] = ((dk[mine] + xrecv[block, 0, part].astype(F32)) * score_scale).astype(BF16)
                stage[3, to] = (dv[mine] + xrecv[block, 1, part].astype(F32)).astype(BF16)
            send_out(block, 1, 4, 1)

        for block in reversed(range(blocks)):
            own = own_span(block)
            inverse = 1.0 / totals[block]
            keep = jnp.where(valid_rows(block), inverse, 0.0)
            grad_t = gbuf[own].T.astype(F32) * keep
            out_t = outt[block]
            delta = jnp.sum(grad_t * out_t, axis=0, keepdims=True) * inverse
            grad_low_t = grad_t.astype(BF16)
            grad_low = grad_t.T.astype(BF16)
            query_now = qbuf[own]
            dq_t = jnp.zeros((HSIZE, rows), F32)
            for index in range(0, block + 1, 2):
                count = min(2, block + 1 - index)
                span = key_span(index, count)
                low = pbuf[p_span(block, index, count)]
                grad_scores = dot(vbuf[span], grad_low_t, (1, 0))
                score_grad = (low.astype(F32) * (grad_scores - delta)).astype(BF16)
                dv_part = dot(low, grad_low, (1, 0))
                dk_part = dot(score_grad, query_now, (1, 0))
                dv[span] = dv_part if block == blocks - 1 else dv[span] + dv_part
                dk[span] = dk_part if block == blocks - 1 else dk[span] + dk_part
                dq_t += dot(kt[:, span], score_grad, (1, 0))
            stage[1, own] = (dq_t * score_scale).T.astype(BF16)
            for unit in range(2):
                theirs = key_rows_of(2 * block + unit, half_of(unit, 1 - core))
                part = pl.ds(unit * half_rows, half_rows)
                xsend[block, 0, part] = dk[theirs].astype(BF16)
                xsend[block, 1, part] = dv[theirs].astype(BF16)
            pltpu.make_async_remote_copy(
                src_ref=xsend.at[block], dst_ref=xrecv.at[block],
                send_sem=xsend_sem, recv_sem=xrecv_sem.at[block],
                device_id={"section": sibling}, device_id_type=MESH,
            ).start()

            if block < blocks - 1:
                finish(block + 1)

        finish(0)

        for kind in (0, 2):
            part = landing[kind].at[pl.ds(0, sections * half_rows)]
            pltpu.make_async_copy(part, part, fsend_sem.at[kind // 2]).wait()
        pltpu.make_async_copy(xsend, xsend, xsend_sem).wait()

        own_rows = sections * half_rows
        for group, (first, last) in enumerate(((0, 1), (1, 4))):
            @pl.when(to_itself)
            def _():
                part = stage.at[pl.ds(first, last - first), pl.ds(0, own_rows - chunk)]
                pltpu.make_async_copy(part, part, osend_sem.at[group]).wait()

            @pl.when(jnp.logical_not(to_itself))
            def _():
                part = stage.at[pl.ds(first, last - first)]
                pltpu.make_async_copy(part, part, osend_sem.at[group]).wait()

    wait_sent(2)
    wait_sent(3)
    for group, (first, last) in enumerate(((0, 1), (1, 4))):
        part = out_ref.at[pl.ds(first, last - first)]
        pltpu.make_async_copy(part, part, orecv_sem.at[group]).wait()


def per_device(query_in, key_in, value_in, out_grad, group_len):
    rows, columns = query_in.shape
    sections, tensors = lax.axis_size("section"), lax.axis_size("tensor")
    heads = columns // HSIZE
    chunk = rows // tensors
    seq_len = rows * sections
    own = seq_len // 2
    blocks = sections // 2
    tiles = blocks * (blocks + 1) // 2
    vmem = pltpu.VMEM
    dma = pltpu.SemaphoreType.DMA
    anywhere = pl.BlockSpec(memory_space=pl.ANY)
    out = pl.pallas_call(
        functools.partial(attention_kernel, sections, tensors, heads),
        out_shape=jax.ShapeDtypeStruct((4, chunk, columns * tensors), BF16),
        in_specs=[pl.BlockSpec(memory_space=pltpu.SMEM)] + [anywhere] * 4,
        out_specs=anywhere,
        scratch_shapes=[
            vmem((seq_len, HSIZE), BF16),
            vmem((seq_len, HSIZE), BF16),
            vmem((own, HSIZE), BF16),
            vmem((own, HSIZE), BF16),
            vmem((HSIZE, seq_len), BF16),
            vmem((HSIZE, seq_len), BF16),
            vmem((seq_len, HSIZE), BF16),
            vmem((rows, HSIZE), BF16),
            vmem((tiles * 2 * rows, rows), F32),
            vmem((tiles * 2 * rows, rows), BF16),
            vmem((blocks, HSIZE, rows), F32),
            vmem((blocks, 8, rows), F32),
            vmem((blocks, 1, rows), F32),
            vmem((seq_len, HSIZE), F32),
            vmem((seq_len, HSIZE), F32),
            vmem((4, own, HSIZE), BF16),
            vmem((blocks, 2, rows, HSIZE), BF16),
            vmem((blocks, 2, rows, HSIZE), BF16),
            dma((4, sections)),
            dma((2, sections)),
            dma((4,)),
            dma((2,)),
            dma,
            dma((blocks,)),
            dma((2,)),
            dma((2,)),
            pltpu.SemaphoreType.REGULAR((tensors.bit_length() - 1,)),
        ],
        compiler_params=pltpu.CompilerParams(
            collective_id=0, has_side_effects=True, vmem_limit_bytes=56 * 1024 * 1024
        ),
        cost_estimate=pl.CostEstimate(
            flops=12 * HSIZE * seq_len * seq_len // 4,
            bytes_accessed=16 * rows * columns,
            transcendentals=seq_len * seq_len // 4,
        ),
    )(group_len, query_in, key_in, value_in, out_grad)
    return tuple(out[index] for index in range(4))


def solution(mesh):
    whole = P(("section", "tensor"), None)
    return jax.shard_map(
        per_device,
        mesh=mesh,
        in_specs=(P("section", "tensor"),) * 4 + (P(),),
        out_specs=(whole,) * 4,
        check_vma=False,
    )
```

```python
import functools
import math

import jax
import jax.numpy as jnp
from jax import lax
from jax.experimental import pallas as pl
from jax.experimental.pallas import tpu as pltpu
from jax.sharding import PartitionSpec as P

HSIZE = 128
CSLOT = 64
NEG_FILL = -1e30
MESH = pl.DeviceIdType.MESH
F32 = jnp.float32
BF16 = jnp.bfloat16


def chip_of(head, tensor, chips):
    if chips != 8:
        return lax.rem(head + tensor, chips)
    level = (head >= 3).astype(jnp.int32)
    return 2 * (head - level + (tensor >> 1) & 3) + level


def section_at(section, step, sections):
    if sections != 16:
        return lax.rem(section + step + 1, sections)
    turn = step >> 2
    shift = jnp.where(turn == 0, 2, jnp.where(turn == 1, 1, jnp.where(turn == 2, 3, 0)))
    return 4 * ((section >> 2) + shift & 3) + (section + step & 3)


def head_at(chip, tensor, chips, heads):
    if chips != 8:
        head = lax.rem(chip - lax.rem(tensor, chips) + chips, chips)
        return (head, head < heads)
    level = chip & 1
    place = (chip >> 1) + 8 - 2 * level - (tensor >> 1) & 3
    return (3 * level + place, place < 3)


def dot(a, b, dims):
    return lax.dot_general(a, b, ((dims[:1], dims[1:]), ((), ())), preferred_element_type=F32)


def attention_kernel(
    sections, tensors, heads,
    len_ref, q_ref, k_ref, v_ref, g_ref, out_ref,
    kbuf, vbuf, qbuf, gbuf, kt, vt, bias, ones, sbuf, pbuf, outt, tops, totals, valid, dk, dv,
    stage, xsend, xrecv,
    recv_sem, fwd_sem, send_sem, fsend_sem, xsend_sem, xrecv_sem, osend_sem, orecv_sem, entered,
):
    rows = q_ref.shape[0]
    half_rows = rows // 2
    chunk = rows // tensors
    half_tensors = tensors // 2
    chips = sections // 2
    blocks = sections // 2
    key_rows = 2 * rows
    score_scale = 1.0 / math.sqrt(HSIZE)
    exp_scale = score_scale * math.log2(math.e)

    me_s = lax.axis_index("section")
    me_t = lax.axis_index("tensor")
    core = me_s & 1
    sibling = me_s + 1 - 2 * core
    head, active = head_at(me_s // 2, me_t, chips, heads)
    inputs = (k_ref, q_ref, v_ref, g_ref)
    landing = (kbuf, qbuf, vbuf, gbuf)

    def aligned(start, size, step):
        return pl.ds(pl.multiple_of(start, step), size)

    def half_of(section, of_core):
        return (of_core + section) & 1

    def key_rows_of(section, half):
        return aligned(section * rows + half * half_rows, half_rows, half_rows)

    def own_rows_of(section):
        return aligned(section * half_rows, half_rows, half_rows)

    def slot(kind, section, half):
        return landing[kind].at[key_rows_of(section, half) if kind in (0, 2) else own_rows_of(section)]

    def group_len_of(group):
        return len_ref[group]

    def p_span(block, index, count=1):
        return pl.ds((block * (block + 1) // 2 + index) * key_rows, count * key_rows)

    def key_span(index, count=1):
        return pl.ds(index * key_rows, count * key_rows)

    def own_span(block):
        return pl.ds(block * rows, rows)

    lane_q = lax.broadcasted_iota(jnp.int32, (1, rows), 1)
    query_place = jnp.where(
        lane_q < half_rows, core * half_rows + lane_q, rows + (1 - core) * half_rows + lane_q - half_rows
    )

    def send_out(first, last, group, block=None):
        column = aligned((me_t * heads + head) * HSIZE, HSIZE, HSIZE)

        @pl.loop(0, sections if block is None else 2)
        def _(step):
            section = section_at(me_s, step, sections) if block is None else 2 * block + step

            @pl.loop(0, half_rows // chunk)
            def _(index):
                tensor = half_of(section, core) * half_tensors + index
                source = stage.at[
                    pl.ds(first, last - first), aligned(section * half_rows + index * chunk, chunk, chunk)
                ]
                place = out_ref.at[pl.ds(first, last - first), :, column]
                itself = jnp.logical_and(section == me_s, tensor == me_t)

                @pl.when(jnp.logical_not(itself))
                def _():
                    pltpu.make_async_remote_copy(
                        src_ref=source, dst_ref=place,
                        send_sem=osend_sem.at[group], recv_sem=orecv_sem.at[group],
                        device_id={"section": section, "tensor": tensor}, device_id_type=MESH,
                    ).start()

                @pl.when(itself)
                def _():
                    pltpu.make_async_copy(source, place, orecv_sem.at[group]).start()

    def valid_rows(block):
        piece = lane_q // CSLOT
        length = jnp.zeros((1, rows), jnp.int32)
        for unit in range(2):
            first = (2 * block + unit) * (rows // CSLOT) + half_of(unit, core) * (half_rows // CSLOT)
            for inner in range(half_rows // CSLOT):
                length = jnp.where(
                    piece == unit * (half_rows // CSLOT) + inner, group_len_of(first + inner), length
                )
        return jnp.where((lane_q & (CSLOT - 1)) < length, 1.0, 0.0).astype(F32)

    barrier = pltpu.get_barrier_semaphore()
    steps = [1 << bit for bit in range(tensors.bit_length() - 1)]
    for step in range(1, sections):
        pl.semaphore_signal(
            barrier, inc=1, device_id={"section": jnp.bitwise_xor(me_s, step)}, device_id_type=MESH
        )
    for step in steps:
        pl.semaphore_signal(
            barrier, inc=1, device_id={"tensor": jnp.bitwise_xor(me_t, step)}, device_id_type=MESH
        )

    @pl.when(active)
    def _():
        lane = lax.broadcasted_iota(jnp.int32, (CSLOT, HSIZE), 1)
        row = lax.broadcasted_iota(jnp.int32, (CSLOT, HSIZE), 0)

        @pl.loop(0, sections * rows // CSLOT)
        def _(group):
            padded = jnp.logical_and(row >= group_len_of(group), lane == 0)
            bias[aligned(group * CSLOT, CSLOT, CSLOT)] = jnp.where(padded, NEG_FILL, 0.0).astype(BF16)

        ones[...] = jnp.where(
            lax.broadcasted_iota(jnp.int32, ones.shape, 1) == 0, 1.0, 0.0
        ).astype(BF16)

        for block in range(blocks):
            valid[block] = valid_rows(block)

    pl.semaphore_wait(barrier, sections - 1 + len(steps))

    def tell(bit):
        if bit < len(steps):
            pl.semaphore_signal(
                entered.at[bit], inc=1, device_id={"tensor": jnp.bitwise_xor(me_t, steps[bit])}, device_id_type=MESH
            )

    def hear(bit):
        if bit < len(steps):
            pl.semaphore_wait(entered.at[bit], 1)
            tell(bit + 1)

    tell(0)

    def send_kind(kind):
        @pl.loop(0, heads)
        def _(step):
            index = lax.rem(step + (me_s >> 1), heads)
            chip = chip_of(index, me_t, chips)
            for half_step in range(2):
                target_core = core if half_step == 0 else 1 - core
                target = 2 * chip + target_core
                half = half_of(me_s, target_core)
                source = inputs[kind].at[
                    aligned(half * half_rows, half_rows, half_rows), aligned(index * HSIZE, HSIZE, HSIZE)
                ]
                place = slot(kind, me_s, half)

                def send():
                    pltpu.make_async_remote_copy(
                        src_ref=source, dst_ref=place,
                        send_sem=send_sem.at[kind], recv_sem=recv_sem.at[kind, me_s],
                        device_id={"section": target}, device_id_type=MESH,
                    ).start()

                if half_step == 0:
                    @pl.when(target != me_s)
                    def _():
                        send()

                    @pl.when(target == me_s)
                    def _():
                        pltpu.make_async_copy(source, place, recv_sem.at[kind, me_s]).start()
                else:
                    send()

    def wait_sent(kind):
        @pl.when(active)
        def _():
            part = vbuf.at[pl.ds(0, (2 * heads - 1) * half_rows)]
            pltpu.make_async_copy(part, part, send_sem.at[kind]).wait()

        @pl.when(jnp.logical_not(active))
        def _():
            part = vbuf.at[pl.ds(0, 2 * heads * half_rows)]
            pltpu.make_async_copy(part, part, send_sem.at[kind]).wait()

    def wait_arrival(kind, section):
        place = slot(kind, section, half_of(section, core))
        pltpu.make_async_copy(place, place, recv_sem.at[kind, section]).wait()

    def forward(kind):
        which = kind // 2

        @pl.loop(0, sections)
        def _(section):
            wait_arrival(kind, section)
            place = slot(kind, section, half_of(section, core))
            pltpu.make_async_remote_copy(
                src_ref=place, dst_ref=place,
                send_sem=fsend_sem.at[which], recv_sem=fwd_sem.at[which, section],
                device_id={"section": sibling}, device_id_type=MESH,
            ).start()

    def wait_forwarded(kind):
        which = kind // 2

        @pl.loop(0, sections)
        def _(section):
            place = slot(kind, section, half_of(section, 1 - core))
            pltpu.make_async_copy(place, place, fwd_sem.at[which, section]).wait()

    send_kind(0)
    send_kind(1)
    wait_sent(0)
    send_kind(2)

    to_itself = me_t < half_tensors

    @pl.when(active)
    def _():
        forward(0)

    hear(0)
    wait_sent(1)
    send_kind(3)

    @pl.when(active)
    def _():
        @pl.loop(0, sections)
        def _(section):
            wait_arrival(1, section)

        wait_forwarded(0)

        for block in range(blocks):
            span = key_span(block)
            kt[:, span] = kbuf[span].T
            query_wide = jnp.concatenate([qbuf[own_span(block)], ones[...]], axis=1)

            top = jnp.full((8, rows), NEG_FILL, F32)
            for index in range(block + 1):
                span = key_span(index)
                key_wide = jnp.concatenate([kbuf[span], bias[span]], axis=1)
                scores = dot(key_wide, query_wide, (1, 1))
                if index == block:
                    place = lax.broadcasted_iota(jnp.int32, (key_rows, rows), 0)
                    scores = jnp.where(place <= query_place, scores, NEG_FILL)
                sbuf[p_span(block, index)] = scores
                top = jnp.maximum(top, jnp.max(scores.reshape(key_rows // 8, 8, rows), axis=0))
            tops[block] = top

        forward(2)

    hear(1)

    @pl.when(active)
    def _():
        wait_forwarded(2)

        for block in range(blocks):
            span = key_span(block)
            vt[:, span] = vbuf[span].T
            shift = jnp.max(tops[block], axis=0, keepdims=True) * exp_scale
            weights = jnp.exp2(sbuf[p_span(block, 0, block + 1)] * exp_scale - shift)
            low = weights.astype(BF16)
            pbuf[p_span(block, 0, block + 1)] = low
            total = jnp.sum(weights, axis=0, keepdims=True)
            totals[block] = total
            out_t = dot(vt[:, key_span(0, block + 1)], low, (1, 0))
            outt[block] = out_t
            stage[0, own_span(block)] = (out_t * (valid[block] / total)).astype(BF16).T

    hear(2)

    @pl.when(active)
    def _():
        send_out(0, 1, 0)

        def finish(block):
            pltpu.make_async_copy(xrecv.at[block], xrecv.at[block], xrecv_sem.at[block]).wait()
            for unit in range(2):
                mine = key_rows_of(2 * block + unit, half_of(unit, core))
                to = aligned(block * rows + unit * half_rows, half_rows, half_rows)
                part = pl.ds(unit * half_rows, half_rows)
                stage[2, to] = ((dk[mine] + xrecv[block, 0, part].astype(F32)) * score_scale).astype(BF16)
                stage[3, to] = (dv[mine] + xrecv[block, 1, part].astype(F32)).astype(BF16)

        def exchange(block):
            for unit in range(2):
                theirs = key_rows_of(2 * block + unit, half_of(unit, 1 - core))
                part = pl.ds(unit * half_rows, half_rows)
                xsend[block, 0, part] = dk[theirs].astype(BF16)
                xsend[block, 1, part] = dv[theirs].astype(BF16)
            pltpu.make_async_remote_copy(
                src_ref=xsend.at[block], dst_ref=xrecv.at[block],
                send_sem=xsend_sem, recv_sem=xrecv_sem.at[block],
                device_id={"section": sibling}, device_id_type=MESH,
            ).start()

        done, waiting, exchanged = [], list(reversed(range(blocks))), []
        for block in list(range(blocks - 1, -1, -2)) + list(range(blocks - 2, -1, -2)):
            own = own_span(block)
            inverse = 1.0 / totals[block]
            wait_arrival(3, 2 * block)
            wait_arrival(3, 2 * block + 1)
            grad_t = gbuf[own].T.astype(F32) * (valid[block] * inverse)
            out_t = outt[block]
            delta = jnp.sum(grad_t * out_t, axis=0, keepdims=True) * inverse
            grad_low_t = grad_t.astype(BF16)
            grad_low = grad_low_t.T
            query_now = qbuf[own]
            dq_t = jnp.zeros((HSIZE, rows), F32)
            for index in range(0, block + 1, 2):
                count = min(2, block + 1 - index)
                span = key_span(index, count)
                low = pbuf[p_span(block, index, count)]
                grad_scores = dot(vbuf[span], grad_low_t, (1, 0))
                score_grad = (low.astype(F32) * (grad_scores - delta)).astype(BF16)
                dv_part = dot(low, grad_low, (1, 0))
                dk_part = dot(score_grad, query_now, (1, 0))
                dv[span] = dv_part if block == blocks - 1 else dv[span] + dv_part
                dk[span] = dk_part if block == blocks - 1 else dk[span] + dk_part
                dq_t += dot(kt[:, span], score_grad, (1, 0))
            stage[1, own] = (dq_t * score_scale).astype(BF16).T
            send_out(1, 2, 1, block)
            for other in exchanged:
                finish(other)
            done.append(block)
            exchanged = [other for other in waiting if all(later in done for later in range(other, blocks))]
            for other in exchanged:
                waiting.remove(other)
                exchange(other)

        for other in exchanged:
            finish(other)

        send_out(2, 4, 2)

        for kind in (0, 2):
            part = landing[kind].at[pl.ds(0, sections * half_rows)]
            pltpu.make_async_copy(part, part, fsend_sem.at[kind // 2]).wait()
        pltpu.make_async_copy(xsend, xsend, xsend_sem).wait()

        own_rows = sections * half_rows
        for group, (first, last) in enumerate(((0, 1), (1, 2), (2, 4))):
            @pl.when(to_itself)
            def _():
                part = stage.at[pl.ds(first, last - first), pl.ds(0, own_rows - chunk)]
                pltpu.make_async_copy(part, part, osend_sem.at[group]).wait()

            @pl.when(jnp.logical_not(to_itself))
            def _():
                part = stage.at[pl.ds(first, last - first)]
                pltpu.make_async_copy(part, part, osend_sem.at[group]).wait()

    wait_sent(2)
    wait_sent(3)
    for group, (first, last) in enumerate(((0, 1), (1, 2), (2, 4))):
        part = out_ref.at[pl.ds(first, last - first)]
        pltpu.make_async_copy(part, part, orecv_sem.at[group]).wait()


def per_device(query_in, key_in, value_in, out_grad, group_len):
    rows, columns = query_in.shape
    sections, tensors = lax.axis_size("section"), lax.axis_size("tensor")
    heads = columns // HSIZE
    chunk = rows // tensors
    seq_len = rows * sections
    own = seq_len // 2
    blocks = sections // 2
    tiles = blocks * (blocks + 1) // 2
    vmem = pltpu.VMEM
    dma = pltpu.SemaphoreType.DMA
    anywhere = pl.BlockSpec(memory_space=pl.ANY)
    out = pl.pallas_call(
        functools.partial(attention_kernel, sections, tensors, heads),
        out_shape=jax.ShapeDtypeStruct((4, chunk, columns * tensors), BF16),
        in_specs=[pl.BlockSpec(memory_space=pltpu.SMEM)] + [anywhere] * 4,
        out_specs=anywhere,
        scratch_shapes=[
            vmem((seq_len, HSIZE), BF16),
            vmem((seq_len, HSIZE), BF16),
            vmem((own, HSIZE), BF16),
            vmem((own, HSIZE), BF16),
            vmem((HSIZE, seq_len), BF16),
            vmem((HSIZE, seq_len), BF16),
            vmem((seq_len, HSIZE), BF16),
            vmem((rows, HSIZE), BF16),
            vmem((tiles * 2 * rows, rows), F32),
            vmem((tiles * 2 * rows, rows), BF16),
            vmem((blocks, HSIZE, rows), F32),
            vmem((blocks, 8, rows), F32),
            vmem((blocks, 1, rows), F32),
            vmem((blocks, 1, rows), F32),
            vmem((seq_len, HSIZE), F32),
            vmem((seq_len, HSIZE), F32),
            vmem((4, own, HSIZE), BF16),
            vmem((blocks, 2, rows, HSIZE), BF16),
            vmem((blocks, 2, rows, HSIZE), BF16),
            dma((4, sections)),
            dma((2, sections)),
            dma((4,)),
            dma((2,)),
            dma,
            dma((blocks,)),
            dma((3,)),
            dma((3,)),
            pltpu.SemaphoreType.REGULAR((tensors.bit_length() - 1,)),
        ],
        compiler_params=pltpu.CompilerParams(
            collective_id=0, has_side_effects=True, vmem_limit_bytes=56 * 1024 * 1024
        ),
        cost_estimate=pl.CostEstimate(
            flops=12 * HSIZE * seq_len * seq_len // 4,
            bytes_accessed=16 * rows * columns,
            transcendentals=seq_len * seq_len // 4,
        ),
    )(group_len, query_in, key_in, value_in, out_grad)
    return tuple(out[index] for index in range(4))


def solution(mesh):
    whole = P(("section", "tensor"), None)
    return jax.shard_map(
        per_device,
        mesh=mesh,
        in_specs=(P("section", "tensor"),) * 4 + (P(),),
        out_specs=(whole,) * 4,
        check_vma=False,
    )
```

```python
import functools
import math

import jax
import jax.numpy as jnp
from jax import lax
from jax.experimental import pallas as pl
from jax.experimental.pallas import tpu as pltpu
from jax.sharding import PartitionSpec as P

HSIZE = 128
CSLOT = 64
NEG_FILL = -1e30
MESH = pl.DeviceIdType.MESH
F32 = jnp.float32
BF16 = jnp.bfloat16


def chip_at(chip, step, chips):
    if chips != 8:
        return lax.rem(chip + step + 1, chips)
    dx, dz = ((2, 1), (2, 0), (1, 1), (3, 1), (1, 0), (3, 0), (0, 1), (0, 0))[step]
    return 2 * ((chip >> 1) + dx & 3) + (chip + dz & 1)


def section_at(section, step, sections):
    if sections != 16:
        return lax.rem(section + step + 1, sections)
    turn = step >> 2
    shift = jnp.where(turn == 0, 2, jnp.where(turn == 1, 1, jnp.where(turn == 2, 3, 0)))
    return 4 * ((section >> 2) + shift & 3) + (section + step & 3)


def head_at(chip, tensor, chips, heads):
    if chips != 8:
        head = lax.rem(chip - lax.rem(tensor, chips) + chips, chips)
        return (head, head < heads)
    level = chip & 1
    place = (chip >> 1) + 8 - 2 * level - (tensor >> 1) & 3
    return (3 * level + place, place < 3)


def dot(a, b, dims):
    return lax.dot_general(a, b, ((dims[:1], dims[1:]), ((), ())), preferred_element_type=F32)


def attention_kernel(
    sections, tensors, heads,
    len_ref, q_ref, k_ref, v_ref, g_ref, out_ref,
    kbuf, vbuf, qbuf, gbuf, kt, vt, bias, ones, sbuf, pbuf, outt, tops, totals, valid, dk, dv,
    stage, xsend, xrecv,
    recv_sem, fwd_sem, send_sem, fsend_sem, xsend_sem, xrecv_sem, osend_sem, orecv_sem, entered,
):
    rows = q_ref.shape[0]
    half_rows = rows // 2
    chunk = rows // tensors
    half_tensors = tensors // 2
    chips = sections // 2
    blocks = sections // 2
    key_rows = 2 * rows
    score_scale = 1.0 / math.sqrt(HSIZE)
    exp_scale = score_scale * math.log2(math.e)

    me_s = lax.axis_index("section")
    me_t = lax.axis_index("tensor")
    core = me_s & 1
    sibling = me_s + 1 - 2 * core
    head, active = head_at(me_s // 2, me_t, chips, heads)
    inputs = (k_ref, q_ref, v_ref, g_ref)
    landing = (kbuf, qbuf, vbuf, gbuf)

    def aligned(start, size, step):
        return pl.ds(pl.multiple_of(start, step), size)

    def half_of(section, of_core):
        return (of_core + section) & 1

    def key_rows_of(section, half):
        return aligned(section * rows + half * half_rows, half_rows, half_rows)

    def own_rows_of(section):
        return aligned(section * half_rows, half_rows, half_rows)

    def slot(kind, section, half):
        return landing[kind].at[key_rows_of(section, half) if kind in (0, 2) else own_rows_of(section)]

    def group_len_of(group):
        return len_ref[group]

    def p_span(block, index, count=1):
        return pl.ds((block * (block + 1) // 2 + index) * key_rows, count * key_rows)

    def key_span(index, count=1):
        return pl.ds(index * key_rows, count * key_rows)

    def own_span(block):
        return pl.ds(block * rows, rows)

    lane_q = lax.broadcasted_iota(jnp.int32, (1, rows), 1)
    query_place = jnp.where(
        lane_q < half_rows, core * half_rows + lane_q, rows + (1 - core) * half_rows + lane_q - half_rows
    )

    def send_out(first, last, group, block=None):
        column = aligned((me_t * heads + head) * HSIZE, HSIZE, HSIZE)

        @pl.loop(0, sections if block is None else 2)
        def _(step):
            section = section_at(me_s, step, sections) if block is None else 2 * block + step

            @pl.loop(0, half_rows // chunk)
            def _(index):
                tensor = half_of(section, core) * half_tensors + index
                source = stage.at[
                    pl.ds(first, last - first), aligned(section * half_rows + index * chunk, chunk, chunk)
                ]
                place = out_ref.at[pl.ds(first, last - first), :, column]
                itself = jnp.logical_and(section == me_s, tensor == me_t)

                @pl.when(jnp.logical_not(itself))
                def _():
                    pltpu.make_async_remote_copy(
                        src_ref=source, dst_ref=place,
                        send_sem=osend_sem.at[group], recv_sem=orecv_sem.at[group],
                        device_id={"section": section, "tensor": tensor}, device_id_type=MESH,
                    ).start()

                @pl.when(itself)
                def _():
                    pltpu.make_async_copy(source, place, orecv_sem.at[group]).start()

    def valid_rows(block):
        piece = lane_q // CSLOT
        length = jnp.zeros((1, rows), jnp.int32)
        for unit in range(2):
            first = (2 * block + unit) * (rows // CSLOT) + half_of(unit, core) * (half_rows // CSLOT)
            for inner in range(half_rows // CSLOT):
                length = jnp.where(
                    piece == unit * (half_rows // CSLOT) + inner, group_len_of(first + inner), length
                )
        return jnp.where((lane_q & (CSLOT - 1)) < length, 1.0, 0.0).astype(F32)

    barrier = pltpu.get_barrier_semaphore()
    steps = [1 << bit for bit in range(tensors.bit_length() - 1)]
    for step in range(1, sections):
        pl.semaphore_signal(
            barrier, inc=1, device_id={"section": jnp.bitwise_xor(me_s, step)}, device_id_type=MESH
        )
    for step in steps:
        pl.semaphore_signal(
            barrier, inc=1, device_id={"tensor": jnp.bitwise_xor(me_t, step)}, device_id_type=MESH
        )

    @pl.when(active)
    def _():
        lane = lax.broadcasted_iota(jnp.int32, (CSLOT, HSIZE), 1)
        row = lax.broadcasted_iota(jnp.int32, (CSLOT, HSIZE), 0)

        @pl.loop(0, sections * rows // CSLOT)
        def _(group):
            padded = jnp.logical_and(row >= group_len_of(group), lane == 0)
            bias[aligned(group * CSLOT, CSLOT, CSLOT)] = jnp.where(padded, NEG_FILL, 0.0).astype(BF16)

        ones[...] = jnp.where(
            lax.broadcasted_iota(jnp.int32, ones.shape, 1) == 0, 1.0, 0.0
        ).astype(BF16)

        for block in range(blocks):
            valid[block] = valid_rows(block)

    pl.semaphore_wait(barrier, sections - 1 + len(steps))

    def tell(bit):
        if bit < len(steps):
            pl.semaphore_signal(
                entered.at[bit], inc=1, device_id={"tensor": jnp.bitwise_xor(me_t, steps[bit])}, device_id_type=MESH
            )

    def hear(bit):
        if bit < len(steps):
            pl.semaphore_wait(entered.at[bit], 1)
            tell(bit + 1)

    tell(0)

    turns = []
    for step in range(chips):
        chip = chip_at(me_s >> 1, step, chips)
        turns.append((chip,) + head_at(chip, me_t, chips, heads))

    def send_kind(kind):
        for step, (chip, index, busy) in enumerate(turns):
            @pl.when(busy)
            def _():
                for half_step in range(2):
                    target_core = core if half_step == 0 else 1 - core
                    half = half_of(me_s, target_core)
                    source = inputs[kind].at[
                        aligned(half * half_rows, half_rows, half_rows), aligned(index * HSIZE, HSIZE, HSIZE)
                    ]
                    place = slot(kind, me_s, half)
                    if step == chips - 1 and half_step == 0:
                        pltpu.make_async_copy(source, place, recv_sem.at[kind, me_s]).start()
                    else:
                        pltpu.make_async_remote_copy(
                            src_ref=source, dst_ref=place,
                            send_sem=send_sem.at[kind], recv_sem=recv_sem.at[kind, me_s],
                            device_id={"section": 2 * chip + target_core}, device_id_type=MESH,
                        ).start()

    def wait_sent(kind):
        @pl.when(active)
        def _():
            part = vbuf.at[pl.ds(0, (2 * heads - 1) * half_rows)]
            pltpu.make_async_copy(part, part, send_sem.at[kind]).wait()

        @pl.when(jnp.logical_not(active))
        def _():
            part = vbuf.at[pl.ds(0, 2 * heads * half_rows)]
            pltpu.make_async_copy(part, part, send_sem.at[kind]).wait()

    def wait_arrival(kind, section):
        place = slot(kind, section, half_of(section, core))
        pltpu.make_async_copy(place, place, recv_sem.at[kind, section]).wait()

    def forward(kind):
        which = kind // 2

        @pl.loop(0, sections)
        def _(section):
            wait_arrival(kind, section)
            place = slot(kind, section, half_of(section, core))
            pltpu.make_async_remote_copy(
                src_ref=place, dst_ref=place,
                send_sem=fsend_sem.at[which], recv_sem=fwd_sem.at[which, section],
                device_id={"section": sibling}, device_id_type=MESH,
            ).start()

    def wait_forwarded(kind):
        which = kind // 2

        @pl.loop(0, sections)
        def _(section):
            place = slot(kind, section, half_of(section, 1 - core))
            pltpu.make_async_copy(place, place, fwd_sem.at[which, section]).wait()

    send_kind(0)
    send_kind(1)
    wait_sent(0)
    send_kind(2)

    to_itself = me_t < half_tensors

    @pl.when(active)
    def _():
        forward(0)

    hear(0)
    wait_sent(1)
    send_kind(3)

    @pl.when(active)
    def _():
        @pl.loop(0, sections)
        def _(section):
            wait_arrival(1, section)

        wait_forwarded(0)

        for block in range(blocks):
            span = key_span(block)
            kt[:, span] = kbuf[span].T
            query_wide = jnp.concatenate([qbuf[own_span(block)], ones[...]], axis=1)

            top = jnp.full((8, rows), NEG_FILL, F32)
            for index in range(block + 1):
                span = key_span(index)
                key_wide = jnp.concatenate([kbuf[span], bias[span]], axis=1)
                scores = dot(key_wide, query_wide, (1, 1))
                if index == block:
                    place = lax.broadcasted_iota(jnp.int32, (key_rows, rows), 0)
                    scores = jnp.where(place <= query_place, scores, NEG_FILL)
                sbuf[p_span(block, index)] = scores
                top = jnp.maximum(top, jnp.max(scores.reshape(key_rows // 8, 8, rows), axis=0))
            tops[block] = top

        forward(2)

    hear(1)

    @pl.when(active)
    def _():
        wait_forwarded(2)

        for block in range(blocks):
            span = key_span(block)
            vt[:, span] = vbuf[span].T
            shift = jnp.max(tops[block], axis=0, keepdims=True) * exp_scale
            weights = jnp.exp2(sbuf[p_span(block, 0, block + 1)] * exp_scale - shift)
            low = weights.astype(BF16)
            pbuf[p_span(block, 0, block + 1)] = low
            total = jnp.sum(weights, axis=0, keepdims=True)
            totals[block] = total
            out_t = dot(vt[:, key_span(0, block + 1)], low, (1, 0))
            outt[block] = out_t
            stage[0, own_span(block)] = (out_t * (valid[block] / total)).astype(BF16).T

    hear(2)

    @pl.when(active)
    def _():
        send_out(0, 1, 0)

        def finish(block):
            pltpu.make_async_copy(xrecv.at[block], xrecv.at[block], xrecv_sem.at[block]).wait()
            for unit in range(2):
                mine = key_rows_of(2 * block + unit, half_of(unit, core))
                to = aligned(block * rows + unit * half_rows, half_rows, half_rows)
                part = pl.ds(unit * half_rows, half_rows)
                stage[2, to] = ((dk[mine] + xrecv[block, 0, part].astype(F32)) * score_scale).astype(BF16)
                stage[3, to] = (dv[mine] + xrecv[block, 1, part].astype(F32)).astype(BF16)

        def exchange(block):
            for unit in range(2):
                theirs = key_rows_of(2 * block + unit, half_of(unit, 1 - core))
                part = pl.ds(unit * half_rows, half_rows)
                xsend[block, 0, part] = dk[theirs].astype(BF16)
                xsend[block, 1, part] = dv[theirs].astype(BF16)
            pltpu.make_async_remote_copy(
                src_ref=xsend.at[block], dst_ref=xrecv.at[block],
                send_sem=xsend_sem, recv_sem=xrecv_sem.at[block],
                device_id={"section": sibling}, device_id_type=MESH,
            ).start()

        done, waiting, exchanged = [], list(reversed(range(blocks))), []
        for block in list(range(blocks - 1, -1, -2)) + list(range(blocks - 2, -1, -2)):
            own = own_span(block)
            inverse = 1.0 / totals[block]
            wait_arrival(3, 2 * block)
            wait_arrival(3, 2 * block + 1)
            grad_t = gbuf[own].T.astype(F32) * (valid[block] * inverse)
            out_t = outt[block]
            delta = jnp.sum(grad_t * out_t, axis=0, keepdims=True) * inverse
            grad_low_t = grad_t.astype(BF16)
            grad_low = grad_low_t.T
            query_now = qbuf[own]
            dq_t = jnp.zeros((HSIZE, rows), F32)
            for index in range(0, block + 1, 2):
                count = min(2, block + 1 - index)
                span = key_span(index, count)
                low = pbuf[p_span(block, index, count)]
                grad_scores = dot(vbuf[span], grad_low_t, (1, 0))
                score_grad = (low.astype(F32) * (grad_scores - delta)).astype(BF16)
                dv_part = dot(low, grad_low, (1, 0))
                dk_part = dot(score_grad, query_now, (1, 0))
                dv[span] = dv_part if block == blocks - 1 else dv[span] + dv_part
                dk[span] = dk_part if block == blocks - 1 else dk[span] + dk_part
                dq_t += dot(kt[:, span], score_grad, (1, 0))
            stage[1, own] = (dq_t * score_scale).astype(BF16).T
            send_out(1, 2, 1, block)
            for other in exchanged:
                finish(other)
            done.append(block)
            exchanged = [other for other in waiting if all(later in done for later in range(other, blocks))]
            for other in exchanged:
                waiting.remove(other)
                exchange(other)

        for other in exchanged:
            finish(other)

        send_out(2, 4, 2)

        for kind in (0, 2):
            part = landing[kind].at[pl.ds(0, sections * half_rows)]
            pltpu.make_async_copy(part, part, fsend_sem.at[kind // 2]).wait()
        pltpu.make_async_copy(xsend, xsend, xsend_sem).wait()

        own_rows = sections * half_rows
        for group, (first, last) in enumerate(((0, 1), (1, 2), (2, 4))):
            @pl.when(to_itself)
            def _():
                part = stage.at[pl.ds(first, last - first), pl.ds(0, own_rows - chunk)]
                pltpu.make_async_copy(part, part, osend_sem.at[group]).wait()

            @pl.when(jnp.logical_not(to_itself))
            def _():
                part = stage.at[pl.ds(first, last - first)]
                pltpu.make_async_copy(part, part, osend_sem.at[group]).wait()

    wait_sent(2)
    wait_sent(3)
    for group, (first, last) in enumerate(((0, 1), (1, 2), (2, 4))):
        part = out_ref.at[pl.ds(first, last - first)]
        pltpu.make_async_copy(part, part, orecv_sem.at[group]).wait()


def split_kernel(out_ref, *refs):
    *parts, held, in_sem, out_sem = refs
    loads = [pltpu.make_async_copy(out_ref.at[index], held.at[index], in_sem.at[index]) for index in range(4)]
    stores = [pltpu.make_async_copy(held.at[index], parts[index], out_sem.at[index]) for index in range(4)]
    for load in loads:
        load.start()
    for load, store in zip(loads, stores):
        load.wait()
        store.start()
    for store in stores:
        store.wait()


def per_device(query_in, key_in, value_in, out_grad, group_len):
    rows, columns = query_in.shape
    sections, tensors = lax.axis_size("section"), lax.axis_size("tensor")
    heads = columns // HSIZE
    chunk = rows // tensors
    seq_len = rows * sections
    own = seq_len // 2
    blocks = sections // 2
    tiles = blocks * (blocks + 1) // 2
    vmem = pltpu.VMEM
    dma = pltpu.SemaphoreType.DMA
    anywhere = pl.BlockSpec(memory_space=pl.ANY)
    out = pl.pallas_call(
        functools.partial(attention_kernel, sections, tensors, heads),
        out_shape=jax.ShapeDtypeStruct((4, chunk, columns * tensors), BF16),
        in_specs=[pl.BlockSpec(memory_space=pltpu.SMEM)] + [anywhere] * 4,
        out_specs=anywhere,
        scratch_shapes=[
            vmem((seq_len, HSIZE), BF16),
            vmem((seq_len, HSIZE), BF16),
            vmem((own, HSIZE), BF16),
            vmem((own, HSIZE), BF16),
            vmem((HSIZE, seq_len), BF16),
            vmem((HSIZE, seq_len), BF16),
            vmem((seq_len, HSIZE), BF16),
            vmem((rows, HSIZE), BF16),
            vmem((tiles * 2 * rows, rows), F32),
            vmem((tiles * 2 * rows, rows), BF16),
            vmem((blocks, HSIZE, rows), F32),
            vmem((blocks, 8, rows), F32),
            vmem((blocks, 1, rows), F32),
            vmem((blocks, 1, rows), F32),
            vmem((seq_len, HSIZE), F32),
            vmem((seq_len, HSIZE), F32),
            vmem((4, own, HSIZE), BF16),
            vmem((blocks, 2, rows, HSIZE), BF16),
            vmem((blocks, 2, rows, HSIZE), BF16),
            dma((4, sections)),
            dma((2, sections)),
            dma((4,)),
            dma((2,)),
            dma,
            dma((blocks,)),
            dma((3,)),
            dma((3,)),
            pltpu.SemaphoreType.REGULAR((tensors.bit_length() - 1,)),
        ],
        compiler_params=pltpu.CompilerParams(
            collective_id=0, has_side_effects=True, vmem_limit_bytes=56 * 1024 * 1024
        ),
        cost_estimate=pl.CostEstimate(
            flops=12 * HSIZE * seq_len * seq_len // 4,
            bytes_accessed=16 * rows * columns,
            transcendentals=seq_len * seq_len // 4,
        ),
    )(group_len, query_in, key_in, value_in, out_grad)
    return pl.pallas_call(
        split_kernel,
        out_shape=[jax.ShapeDtypeStruct(out.shape[1:], BF16)] * 4,
        in_specs=[anywhere],
        out_specs=[anywhere] * 4,
        scratch_shapes=[vmem(out.shape, BF16), dma((4,)), dma((4,))],
    )(out)


def solution(mesh):
    whole = P(("section", "tensor"), None)
    return jax.shard_map(
        per_device,
        mesh=mesh,
        in_specs=(P("section", "tensor"),) * 4 + (P(),),
        out_specs=(whole,) * 4,
        check_vma=False,
    )
```

```python
import functools
import math

import jax
import jax.numpy as jnp
from jax import lax
from jax.experimental import pallas as pl
from jax.experimental.pallas import tpu as pltpu
from jax.sharding import PartitionSpec as P

HSIZE = 128
CSLOT = 64
NEG_FILL = -1e30
MESH = pl.DeviceIdType.MESH
F32 = jnp.float32
BF16 = jnp.bfloat16


def chip_at(chip, step, chips):
    if chips != 8:
        return lax.rem(chip + step + 1, chips)
    dx, dz = ((2, 1), (2, 0), (1, 1), (3, 1), (1, 0), (3, 0), (0, 1), (0, 0))[step]
    return 2 * ((chip >> 1) + dx & 3) + (chip + dz & 1)


def section_at(section, step, sections):
    if sections != 16:
        return lax.rem(section + step + 1, sections)
    turn = step >> 2
    shift = jnp.where(turn == 0, 2, jnp.where(turn == 1, 1, jnp.where(turn == 2, 3, 0)))
    return 4 * ((section >> 2) + shift & 3) + (section + step & 3)


def head_at(chip, tensor, chips, heads):
    if chips != 8:
        head = lax.rem(chip - lax.rem(tensor, chips) + chips, chips)
        return (head, head < heads)
    level = chip & 1
    place = (chip >> 1) + 8 - 2 * level - (tensor >> 1) & 3
    return (3 * level + place, place < 3)


def dot(a, b, dims):
    return lax.dot_general(a, b, ((dims[:1], dims[1:]), ((), ())), preferred_element_type=F32)


def attention_kernel(
    sections, tensors, heads,
    len_ref, q_ref, k_ref, v_ref, g_ref, out_ref,
    kbuf, vbuf, qbuf, gbuf, kt, vt, bias, ones, sbuf, pbuf, outt, tops, totals, valid, dk, dv,
    stage, xsend, xrecv,
    recv_sem, fwd_sem, send_sem, fsend_sem, xsend_sem, xrecv_sem, osend_sem, orecv_sem, entered,
):
    rows = q_ref.shape[0]
    half_rows = rows // 2
    chunk = rows // tensors
    half_tensors = tensors // 2
    chips = sections // 2
    blocks = sections // 2
    key_rows = 2 * rows
    score_scale = 1.0 / math.sqrt(HSIZE)
    exp_scale = score_scale * math.log2(math.e)

    me_s = lax.axis_index("section")
    me_t = lax.axis_index("tensor")
    core = me_s & 1
    sibling = me_s + 1 - 2 * core
    head, active = head_at(me_s // 2, me_t, chips, heads)
    inputs = (k_ref, q_ref, v_ref, g_ref)
    landing = (kbuf, qbuf, vbuf, gbuf)

    def aligned(start, size, step):
        return pl.ds(pl.multiple_of(start, step), size)

    def half_of(section, of_core):
        return (of_core + section) & 1

    def key_rows_of(section, half):
        return aligned(section * rows + half * half_rows, half_rows, half_rows)

    def own_rows_of(section):
        return aligned(section * half_rows, half_rows, half_rows)

    def slot(kind, section, half):
        return landing[kind].at[key_rows_of(section, half) if kind in (0, 2) else own_rows_of(section)]

    def group_len_of(group):
        return len_ref[group]

    def p_span(block, index, count=1):
        return pl.ds((block * (block + 1) // 2 + index) * key_rows, count * key_rows)

    def key_span(index, count=1):
        return pl.ds(index * key_rows, count * key_rows)

    def own_span(block):
        return pl.ds(block * rows, rows)

    lane_q = lax.broadcasted_iota(jnp.int32, (1, rows), 1)
    query_place = jnp.where(
        lane_q < half_rows, core * half_rows + lane_q, rows + (1 - core) * half_rows + lane_q - half_rows
    )

    def send_out(first, last, group, block=None):
        column = aligned((me_t * heads + head) * HSIZE, HSIZE, HSIZE)

        @pl.loop(0, sections if block is None else 2)
        def _(step):
            section = section_at(me_s, step, sections) if block is None else 2 * block + step

            @pl.loop(0, half_rows // chunk)
            def _(index):
                tensor = half_of(section, core) * half_tensors + index
                source = stage.at[
                    pl.ds(first, last - first), aligned(section * half_rows + index * chunk, chunk, chunk)
                ]
                place = out_ref.at[pl.ds(first, last - first), :, column]
                itself = jnp.logical_and(section == me_s, tensor == me_t)

                @pl.when(jnp.logical_not(itself))
                def _():
                    pltpu.make_async_remote_copy(
                        src_ref=source, dst_ref=place,
                        send_sem=osend_sem.at[group], recv_sem=orecv_sem.at[group],
                        device_id={"section": section, "tensor": tensor}, device_id_type=MESH,
                    ).start()

                @pl.when(itself)
                def _():
                    pltpu.make_async_copy(source, place, orecv_sem.at[group]).start()

    def valid_rows(block):
        piece = lane_q // CSLOT
        length = jnp.zeros((1, rows), jnp.int32)
        for unit in range(2):
            first = (2 * block + unit) * (rows // CSLOT) + half_of(unit, core) * (half_rows // CSLOT)
            for inner in range(half_rows // CSLOT):
                length = jnp.where(
                    piece == unit * (half_rows // CSLOT) + inner, group_len_of(first + inner), length
                )
        return jnp.where((lane_q & (CSLOT - 1)) < length, 1.0, 0.0).astype(F32)

    barrier = pltpu.get_barrier_semaphore()
    steps = [1 << bit for bit in range(tensors.bit_length() - 1)]
    for step in range(1, sections):
        pl.semaphore_signal(
            barrier, inc=1, device_id={"section": jnp.bitwise_xor(me_s, step)}, device_id_type=MESH
        )
    for step in steps:
        pl.semaphore_signal(
            barrier, inc=1, device_id={"tensor": jnp.bitwise_xor(me_t, step)}, device_id_type=MESH
        )

    @pl.when(active)
    def _():
        lane = lax.broadcasted_iota(jnp.int32, (CSLOT, HSIZE), 1)
        row = lax.broadcasted_iota(jnp.int32, (CSLOT, HSIZE), 0)

        @pl.loop(0, sections * rows // CSLOT)
        def _(group):
            padded = jnp.logical_and(row >= group_len_of(group), lane == 0)
            bias[aligned(group * CSLOT, CSLOT, CSLOT)] = jnp.where(padded, NEG_FILL, 0.0).astype(BF16)

        ones[...] = jnp.where(
            lax.broadcasted_iota(jnp.int32, ones.shape, 1) == 0, 1.0, 0.0
        ).astype(BF16)

        for block in range(blocks):
            valid[block] = valid_rows(block)

    pl.semaphore_wait(barrier, sections - 1 + len(steps))

    def tell(bit):
        if bit < len(steps):
            pl.semaphore_signal(
                entered.at[bit], inc=1, device_id={"tensor": jnp.bitwise_xor(me_t, steps[bit])}, device_id_type=MESH
            )

    def hear(bit):
        if bit < len(steps):
            pl.semaphore_wait(entered.at[bit], 1)
            tell(bit + 1)

    tell(0)

    turns = []
    for step in range(chips):
        chip = chip_at(me_s >> 1, step, chips)
        turns.append((chip,) + head_at(chip, me_t, chips, heads))

    def send_kind(kind):
        for step, (chip, index, busy) in enumerate(turns):
            @pl.when(busy)
            def _():
                for half_step in range(2):
                    target_core = core if half_step == 0 else 1 - core
                    half = half_of(me_s, target_core)
                    source = inputs[kind].at[
                        aligned(half * half_rows, half_rows, half_rows), aligned(index * HSIZE, HSIZE, HSIZE)
                    ]
                    place = slot(kind, me_s, half)
                    if step == chips - 1 and half_step == 0:
                        pltpu.make_async_copy(source, place, recv_sem.at[kind, me_s]).start()
                    else:
                        pltpu.make_async_remote_copy(
                            src_ref=source, dst_ref=place,
                            send_sem=send_sem.at[kind], recv_sem=recv_sem.at[kind, me_s],
                            device_id={"section": 2 * chip + target_core}, device_id_type=MESH,
                        ).start()

    def wait_sent(kind):
        @pl.when(active)
        def _():
            part = vbuf.at[pl.ds(0, (2 * heads - 1) * half_rows)]
            pltpu.make_async_copy(part, part, send_sem.at[kind]).wait()

        @pl.when(jnp.logical_not(active))
        def _():
            part = vbuf.at[pl.ds(0, 2 * heads * half_rows)]
            pltpu.make_async_copy(part, part, send_sem.at[kind]).wait()

    def wait_arrival(kind, section):
        place = slot(kind, section, half_of(section, core))
        pltpu.make_async_copy(place, place, recv_sem.at[kind, section]).wait()

    def forward(kind):
        which = kind // 2

        @pl.loop(0, sections)
        def _(section):
            wait_arrival(kind, section)
            place = slot(kind, section, half_of(section, core))
            pltpu.make_async_remote_copy(
                src_ref=place, dst_ref=place,
                send_sem=fsend_sem.at[which], recv_sem=fwd_sem.at[which, section],
                device_id={"section": sibling}, device_id_type=MESH,
            ).start()

    def wait_forwarded(kind):
        which = kind // 2

        @pl.loop(0, sections)
        def _(section):
            place = slot(kind, section, half_of(section, 1 - core))
            pltpu.make_async_copy(place, place, fwd_sem.at[which, section]).wait()

    send_kind(0)
    send_kind(1)
    wait_sent(0)
    send_kind(2)

    to_itself = me_t < half_tensors

    @pl.when(active)
    def _():
        forward(0)

    hear(0)
    wait_sent(1)
    send_kind(3)

    @pl.when(active)
    def _():
        @pl.loop(0, sections)
        def _(section):
            wait_arrival(1, section)

        wait_forwarded(0)

        for block in range(blocks):
            span = key_span(block)
            kt[:, span] = kbuf[span].T
            query_wide = jnp.concatenate([qbuf[own_span(block)], ones[...]], axis=1)

            top = jnp.full((8, rows), NEG_FILL, F32)
            for index in range(block + 1):
                span = key_span(index)
                key_wide = jnp.concatenate([kbuf[span], bias[span]], axis=1)
                scores = dot(key_wide, query_wide, (1, 1))
                if index == block:
                    place = lax.broadcasted_iota(jnp.int32, (key_rows, rows), 0)
                    scores = jnp.where(place <= query_place, scores, NEG_FILL)
                sbuf[p_span(block, index)] = scores
                top = jnp.maximum(top, jnp.max(scores.reshape(key_rows // 8, 8, rows), axis=0))
            tops[block] = top

        forward(2)

    hear(1)

    @pl.when(active)
    def _():
        wait_forwarded(2)

        for block in range(blocks):
            span = key_span(block)
            vt[:, span] = vbuf[span].T
            shift = jnp.max(tops[block], axis=0, keepdims=True) * exp_scale
            weights = jnp.exp2(sbuf[p_span(block, 0, block + 1)] * exp_scale - shift)
            low = weights.astype(BF16)
            pbuf[p_span(block, 0, block + 1)] = low
            total = jnp.sum(weights, axis=0, keepdims=True)
            totals[block] = total
            out_t = dot(vt[:, key_span(0, block + 1)], low, (1, 0))
            outt[block] = out_t
            stage[0, own_span(block)] = (out_t * (valid[block] / total)).astype(BF16).T

    hear(2)

    @pl.when(active)
    def _():
        send_out(0, 1, 0)

        def finish(block):
            pltpu.make_async_copy(xrecv.at[block], xrecv.at[block], xrecv_sem.at[block]).wait()
            for unit in range(2):
                mine = key_rows_of(2 * block + unit, half_of(unit, core))
                to = aligned(block * rows + unit * half_rows, half_rows, half_rows)
                part = pl.ds(unit * half_rows, half_rows)
                stage[2, to] = ((dk[mine] + xrecv[block, 0, part].astype(F32)) * score_scale).astype(BF16)
                stage[3, to] = (dv[mine] + xrecv[block, 1, part].astype(F32)).astype(BF16)

        def exchange(block):
            for unit in range(2):
                theirs = key_rows_of(2 * block + unit, half_of(unit, 1 - core))
                part = pl.ds(unit * half_rows, half_rows)
                xsend[block, 0, part] = dk[theirs].astype(BF16)
                xsend[block, 1, part] = dv[theirs].astype(BF16)
            pltpu.make_async_remote_copy(
                src_ref=xsend.at[block], dst_ref=xrecv.at[block],
                send_sem=xsend_sem, recv_sem=xrecv_sem.at[block],
                device_id={"section": sibling}, device_id_type=MESH,
            ).start()

        done, waiting, exchanged = [], list(reversed(range(blocks))), []
        for block in list(range(blocks - 1, -1, -2)) + list(range(blocks - 2, -1, -2)):
            own = own_span(block)
            inverse = 1.0 / totals[block]
            wait_arrival(3, 2 * block)
            wait_arrival(3, 2 * block + 1)
            grad_t = gbuf[own].T.astype(F32) * (valid[block] * inverse)
            out_t = outt[block]
            delta = jnp.sum(grad_t * out_t, axis=0, keepdims=True) * inverse
            grad_low_t = grad_t.astype(BF16)
            grad_low = grad_low_t.T
            query_now = qbuf[own]
            dq_t = jnp.zeros((HSIZE, rows), F32)
            for index in range(0, block + 1, 2):
                count = min(2, block + 1 - index)
                span = key_span(index, count)
                low = pbuf[p_span(block, index, count)]
                grad_scores = dot(vbuf[span], grad_low_t, (1, 0))
                score_grad = (low.astype(F32) * (grad_scores - delta)).astype(BF16)
                dv_part = dot(low, grad_low, (1, 0))
                dk_part = dot(score_grad, query_now, (1, 0))
                dv[span] = dv_part if block == blocks - 1 else dv[span] + dv_part
                dk[span] = dk_part if block == blocks - 1 else dk[span] + dk_part
                dq_t += dot(kt[:, span], score_grad, (1, 0))
            done.append(block)
            ready = [other for other in waiting if all(later in done for later in range(other, blocks))]
            for other in ready:
                waiting.remove(other)
                exchange(other)
            stage[1, own] = (dq_t * score_scale).astype(BF16).T
            send_out(1, 2, 1, block)
            for other in exchanged:
                finish(other)
            exchanged = ready

        for other in exchanged:
            finish(other)

        send_out(2, 4, 2)

        for kind in (0, 2):
            part = landing[kind].at[pl.ds(0, sections * half_rows)]
            pltpu.make_async_copy(part, part, fsend_sem.at[kind // 2]).wait()
        pltpu.make_async_copy(xsend, xsend, xsend_sem).wait()

        own_rows = sections * half_rows
        for group, (first, last) in enumerate(((0, 1), (1, 2), (2, 4))):
            @pl.when(to_itself)
            def _():
                part = stage.at[pl.ds(first, last - first), pl.ds(0, own_rows - chunk)]
                pltpu.make_async_copy(part, part, osend_sem.at[group]).wait()

            @pl.when(jnp.logical_not(to_itself))
            def _():
                part = stage.at[pl.ds(first, last - first)]
                pltpu.make_async_copy(part, part, osend_sem.at[group]).wait()

    wait_sent(2)
    wait_sent(3)
    for group, (first, last) in enumerate(((0, 1), (1, 2), (2, 4))):
        part = out_ref.at[pl.ds(first, last - first)]
        pltpu.make_async_copy(part, part, orecv_sem.at[group]).wait()


def split_kernel(out_ref, *refs):
    *parts, held, in_sem, out_sem = refs
    loads = [pltpu.make_async_copy(out_ref.at[index], held.at[index], in_sem.at[index]) for index in range(4)]
    stores = [pltpu.make_async_copy(held.at[index], parts[index], out_sem.at[index]) for index in range(4)]
    for load in loads:
        load.start()
    for load, store in zip(loads, stores):
        load.wait()
        store.start()
    for store in stores:
        store.wait()


def per_device(query_in, key_in, value_in, out_grad, group_len):
    rows, columns = query_in.shape
    sections, tensors = lax.axis_size("section"), lax.axis_size("tensor")
    heads = columns // HSIZE
    chunk = rows // tensors
    seq_len = rows * sections
    own = seq_len // 2
    blocks = sections // 2
    tiles = blocks * (blocks + 1) // 2
    vmem = pltpu.VMEM
    dma = pltpu.SemaphoreType.DMA
    anywhere = pl.BlockSpec(memory_space=pl.ANY)
    out = pl.pallas_call(
        functools.partial(attention_kernel, sections, tensors, heads),
        out_shape=jax.ShapeDtypeStruct((4, chunk, columns * tensors), BF16),
        in_specs=[pl.BlockSpec(memory_space=pltpu.SMEM)] + [anywhere] * 4,
        out_specs=anywhere,
        scratch_shapes=[
            vmem((seq_len, HSIZE), BF16),
            vmem((seq_len, HSIZE), BF16),
            vmem((own, HSIZE), BF16),
            vmem((own, HSIZE), BF16),
            vmem((HSIZE, seq_len), BF16),
            vmem((HSIZE, seq_len), BF16),
            vmem((seq_len, HSIZE), BF16),
            vmem((rows, HSIZE), BF16),
            vmem((tiles * 2 * rows, rows), F32),
            vmem((tiles * 2 * rows, rows), BF16),
            vmem((blocks, HSIZE, rows), F32),
            vmem((blocks, 8, rows), F32),
            vmem((blocks, 1, rows), F32),
            vmem((blocks, 1, rows), F32),
            vmem((seq_len, HSIZE), F32),
            vmem((seq_len, HSIZE), F32),
            vmem((4, own, HSIZE), BF16),
            vmem((blocks, 2, rows, HSIZE), BF16),
            vmem((blocks, 2, rows, HSIZE), BF16),
            dma((4, sections)),
            dma((2, sections)),
            dma((4,)),
            dma((2,)),
            dma,
            dma((blocks,)),
            dma((3,)),
            dma((3,)),
            pltpu.SemaphoreType.REGULAR((tensors.bit_length() - 1,)),
        ],
        compiler_params=pltpu.CompilerParams(
            collective_id=0, has_side_effects=True, vmem_limit_bytes=56 * 1024 * 1024
        ),
        cost_estimate=pl.CostEstimate(
            flops=12 * HSIZE * seq_len * seq_len // 4,
            bytes_accessed=16 * rows * columns,
            transcendentals=seq_len * seq_len // 4,
        ),
    )(group_len, query_in, key_in, value_in, out_grad)
    return pl.pallas_call(
        split_kernel,
        out_shape=[jax.ShapeDtypeStruct(out.shape[1:], BF16)] * 4,
        in_specs=[anywhere],
        out_specs=[anywhere] * 4,
        scratch_shapes=[vmem(out.shape, BF16), dma((4,)), dma((4,))],
    )(out)


def solution(mesh):
    whole = P(("section", "tensor"), None)
    return jax.shard_map(
        per_device,
        mesh=mesh,
        in_specs=(P("section", "tensor"),) * 4 + (P(),),
        out_specs=(whole,) * 4,
        check_vma=False,
    )
```
